512 devices in a mesh: gx: 32 (over y, x, core), yz: 16 (over z).
Axes of the slice: x: 4, y: 4, z: 16, core: 2. Of those that a mesh axis runs over, the one named last changes fastest.
Arguments:
- jitter: float32 [32, 48, 3, 512], P('gx', 'yz'), may hold values from -0.15 to 0.15
- displacement: float32 [32, 48, 3, 512], P('gx', 'yz'), may hold values from -0.1 to 0.1
- volume: float32 [32, 48, 512], P('gx', 'yz'), may hold values from 0.5 to 2
- body_force: float32 [32, 48, 3, 512], P('gx', 'yz'), may hold values from -6 to 6
- phase: int32 [32, 48, 512], P('gx', 'yz'), may hold values from 0 to 2
- counts: int32 [32, 48], replicated, may hold values from 0 to 512, as said below
- pair_list: int32 [13824, 2], P(('gx', 'yz')), may hold values from 0 to 143, as said below
- pair_live: int32 [13824], P(('gx', 'yz')), may hold values from 0 to 1, as said below
Outputs:
- residual: float32 [32, 48, 3, 512], P('gx', 'yz')
The draws below stay inside these ranges and needn't reach their ends.
Inputs may be any that keep to these rules, and one draw needn't show every extreme that they name: 0 marks an empty block; points 0 to counts - 1 of a block are live. `pair_list`: column 0 is c_i, column 1 is k = (a_j - g + 1) * 48 + c_j; a live entry names two blocks with points whose length and cross-section positions differ by at most one, inside the slab; every such ordered pair whose first block lies in column g is listed exactly once among the entries of column g; a padding entry holds (0, 48). `pair_live`: on each device the live entries come first.
All inputs are finite; a program needn't handle non-finite values.
Results may differ from the reference program's by a relative error of at most 0.0003.
Values sent between devices are 32-bit elements; how exact they have to be, the bound alone decides.
No kernel may reach another device: no remote copies, remote signals or barrier semaphores. Data moves between devices by JAX's collectives and lax.ppermute only.
A program may use at most 64 MiB of HBM per device.

```python
import math
import jax
import jax.numpy as jnp
from jax import lax

BS = 8
PTS = 512
NBX = 32
CS = 48
PAIRS_DEV = 27
N_YZ = 16


def block_tables(key):
    block_kinds = jax.random.randint(jax.random.fold_in(key, 11), (NBX, CS), 0, 8)
    partial_fill = jax.random.randint(jax.random.fold_in(key, 12), (NBX, CS), 1, PTS)
    filled = jnp.where(block_kinds == 0, 0, jnp.where(block_kinds >= 6, partial_fill, PTS)).astype(jnp.int32)
    candidate = jnp.arange(9 * CS, dtype=jnp.int32)
    first_cross = candidate // 9
    neighbour = candidate % 9
    length_step = neighbour // 3 - 1
    cross_step = neighbour % 3 - 1
    shuffle_key = jax.random.fold_in(key, 13)

    def column_tables(position):
        other_length = position + length_step
        other_cross = first_cross + cross_step
        inside = (other_length >= 0) & (other_length < NBX) & (other_cross >= 0) & (other_cross < CS)
        count_first = filled[position, first_cross]
        count_other = filled[jnp.clip(other_length, 0, NBX - 1), jnp.clip(other_cross, 0, CS - 1)]
        usable = (inside & (count_first > 0) & (count_other > 0)).astype(jnp.int32)
        first_entry = jnp.where(usable == 1, first_cross, 0)
        second_entry = jnp.where(usable == 1, (length_step + 1) * CS + other_cross, CS)
        shuffle = jax.random.permutation(jax.random.fold_in(shuffle_key, position), 9 * CS)
        usable = usable[shuffle].reshape(N_YZ, PAIRS_DEV)
        first_entry = first_entry[shuffle].reshape(N_YZ, PAIRS_DEV)
        second_entry = second_entry[shuffle].reshape(N_YZ, PAIRS_DEV)
        ranking_key = (1 - usable) * PAIRS_DEV + jnp.arange(PAIRS_DEV, dtype=jnp.int32)[None, :]
        ranked = jnp.argsort(ranking_key, axis=1)
        usable = jnp.take_along_axis(usable, ranked, axis=1)
        first_entry = jnp.take_along_axis(first_entry, ranked, axis=1)
        second_entry = jnp.take_along_axis(second_entry, ranked, axis=1)
        return (jnp.stack([first_entry, second_entry], axis=-1), usable)
    pair_tables, live_tables = jax.vmap(column_tables)(jnp.arange(NBX, dtype=jnp.int32))
    return (filled, pair_tables.reshape(NBX * 9 * CS, 2).astype(jnp.int32), live_tables.reshape(NBX * 9 * CS).astype(jnp.int32))


def draw_counts(key, part):
    tables = block_tables(key)
    return tables[0]


def draw_pair_list(key, part):
    tables = block_tables(key)
    return tables[1]


def draw_pair_live(key, part):
    tables = block_tables(key)
    return tables[2]


def draw_phase(key, part):
    key = jax.random.fold_in(key, 5)
    phase_roll = jax.random.randint(jax.random.fold_in(key, 1), (NBX, CS, PTS), 0, 4)
    minor_phase = jax.random.randint(jax.random.fold_in(key, 2), (NBX, CS, PTS), 1, 3)
    return jnp.where(phase_roll == 0, minor_phase, 0).astype(jnp.int32)


def levels(key, extent, shards, smallest, high):
    factor_of, own = 1.0, jax.random.fold_in(key, 6)
    for dim, shards_of in shards:
        draws = jnp.exp(jax.random.uniform(jax.random.fold_in(own, dim), (shards_of,), jnp.float32, smallest / len(shards), high / len(shards)))
        factor_of = factor_of * jnp.repeat(draws, extent[dim] // shards_of).reshape([-1 if axis == dim else 1 for axis in range(len(extent))])
    return factor_of


def centred(rng, dims, deviation, most, cuts=(), held_as=jnp.bfloat16):
    array = jax.random.normal(rng, dims, jnp.float32) * deviation
    if len(cuts) > 0:
        array = levels(rng, dims, cuts, -0.22, 0.18) * array
    return jnp.clip(array, min=-most, max=most).astype(held_as)


def setup_inputs(seed: int = 0) -> dict:
    seeds = jax.random.split(jax.random.key(seed), 9)
    jitter = jnp.clip(jax.random.uniform(seeds[0], (NBX, CS, 3, PTS), jnp.float32, -0.15, 0.15) * levels(seeds[0], (NBX, CS, 3, PTS), ((0, 32), (1, 16)), -0.4, 0.0), -0.15, 0.15)
    displacement = jnp.clip(jax.random.uniform(seeds[1], (NBX, CS, 3, PTS), jnp.float32, -0.1, 0.1) * levels(seeds[1], (NBX, CS, 3, PTS), ((0, 32), (1, 16)), -0.4, 0.0), -0.1, 0.1)
    volume = jnp.clip(jnp.exp(math.log(2.0) - 1.3862944 * jax.random.uniform(seeds[2], (NBX, CS, PTS), jnp.float32) ** levels(seeds[2], (NBX, CS, PTS), ((0, 32), (1, 16)), -0.2, 0.2)), 0.5, 2.0)
    body_force = centred(seeds[3], (NBX, CS, 3, PTS), 1.0, 6.0, ((0, 32), (1, 16)), jnp.float32)
    phase = draw_phase(jax.random.fold_in(seeds[8], 71), 0)
    counts = draw_counts(jax.random.fold_in(seeds[8], 71), 0)
    pair_list = draw_pair_list(jax.random.fold_in(seeds[8], 71), 0)
    pair_live = draw_pair_live(jax.random.fold_in(seeds[8], 71), 0)
    return dict(jitter=jitter, displacement=displacement, volume=volume, body_force=body_force, phase=phase, counts=counts, pair_list=pair_list, pair_live=pair_live)


bulk_modulus = 60.0
shear_modulus = 15.0
horizon = 3.0

def lattice(block_side):
    point_index = jnp.arange(block_side * block_side * block_side, dtype=jnp.int32)
    coordinates = jnp.stack([point_index // (block_side * block_side), point_index // block_side % block_side, point_index % block_side])
    return coordinates.astype(jnp.float32)

def tile_valid(alive_first, alive_second, same_block, pair_flag):
    point_total = alive_first.shape[0]
    diagonal = (jnp.arange(point_total, dtype=jnp.int32)[:, None] == jnp.arange(point_total, dtype=jnp.int32)[None, :]).astype(jnp.float32)
    self_bonds = same_block * diagonal
    return (alive_first[:, None] * alive_second[None, :] * (1.0 - self_bonds) * pair_flag, self_bonds)

def bond_terms(lattice_points, offset, fields_first, fields_second, valid_bonds):
    reference_parts = []
    current_parts = []
    for component in range(3):
        base_shift = offset[component] + (lattice_points[component][None, :] - lattice_points[component][:, None])
        reference_part = base_shift + (fields_second[component][None, :] - fields_first[component][:, None])
        current_part = reference_part + (fields_second[3 + component][None, :] - fields_first[3 + component][:, None])
        reference_parts.append(reference_part)
        current_parts.append(current_part)
    reach = jnp.sqrt(jnp.square(reference_parts[0]) + jnp.square(reference_parts[1]) + jnp.square(reference_parts[2]))
    length = jnp.sqrt(jnp.square(current_parts[0]) + jnp.square(current_parts[1]) + jnp.square(current_parts[2]))
    stretch = length - reach
    phase_match = (fields_first[7][:, None] == fields_second[7][None, :]).astype(jnp.float32)
    weight = valid_bonds * phase_match * jnp.square(jnp.maximum(1.0 - reach / horizon, 0.0)) * fields_second[6][None, :]
    return (reach, length, stretch, weight, current_parts)

def first_terms(lattice_points, offset, fields_first, fields_second, valid_bonds):
    reach, length, stretch, weight, current_parts = bond_terms(lattice_points, offset, fields_first, fields_second, valid_bonds)
    return (lax.optimization_barrier(jnp.sum(weight * reach * reach, axis=1)), lax.optimization_barrier(jnp.sum(weight * reach * stretch, axis=1)))

def second_terms(lattice_points, offset, fields_first, fields_second, valid_bonds, self_bonds, state_first, state_second):
    reach, length, stretch, weight, current_parts = bond_terms(lattice_points, offset, fields_first, fields_second, valid_bonds)
    theta_first = state_first[0][:, None]
    kappa_first = state_first[1][:, None]
    theta_second = state_second[0][None, :]
    kappa_second = state_second[1][None, :]
    coefficient = 3.0 * bulk_modulus * reach * (theta_first * kappa_first + theta_second * kappa_second) + 15.0 * shear_modulus * (kappa_first * (stretch - theta_first * reach / 3.0) + kappa_second * (stretch - theta_second * reach / 3.0))
    scaled = weight * coefficient / (length + self_bonds)
    return jnp.stack([lax.optimization_barrier(jnp.sum(scaled * current_parts[0], axis=1)), lax.optimization_barrier(jnp.sum(scaled * current_parts[1], axis=1)), lax.optimization_barrier(jnp.sum(scaled * current_parts[2], axis=1))])

def reference(jitter, displacement, volume, body_force, phase, counts, pair_list, pair_live):
    lattice_points = lattice(BS)
    all_fields = jnp.concatenate([jitter, displacement, volume[:, :, None, :], phase[:, :, None, :].astype(jnp.float32)], axis=2)
    length_blocks = all_fields.shape[0]
    cross_count = all_fields.shape[1]
    points = all_fields.shape[3]
    alive_points = (jnp.arange(points, dtype=jnp.int32)[None, None, :] < counts[:, :, None]).astype(jnp.float32)
    entries = pair_list.shape[0]
    owner_column = jnp.arange(entries, dtype=jnp.int32) // PAIRS_DEV // N_YZ
    first_block = pair_list[:, 0].astype(jnp.int32)
    second_block = pair_list[:, 1].astype(jnp.int32)
    second_length = jnp.clip(owner_column + second_block // cross_count - 1, 0, length_blocks - 1)
    second_cross = second_block % cross_count
    same_flags = (second_block == cross_count + first_block).astype(jnp.float32)
    live_flags = pair_live.astype(jnp.float32)
    offsets = jnp.stack([(second_block // cross_count - 1).astype(jnp.float32) * BS, (second_cross - first_block).astype(jnp.float32) * BS, jnp.zeros((entries,), jnp.float32)], axis=1)
    group_count = entries // 9

    def regroup(values):
        return values.reshape((group_count, 9) + values.shape[1:])
    packed = (regroup(owner_column), regroup(first_block), regroup(second_length), regroup(second_cross), regroup(same_flags), regroup(live_flags), regroup(offsets))

    def first_pass(carried, scan_item):
        own_length, own_cross, other_length, other_cross, same_part, live_part, offset_part = scan_item

        def tile_first(offset, fields_first, fields_second, alive_first, alive_second, same_block, pair_flag):
            valid_bonds, self_bonds = tile_valid(alive_first, alive_second, same_block, pair_flag)
            return first_terms(lattice_points, offset, fields_first, fields_second, valid_bonds)
        mass_part, spread_part = jax.vmap(tile_first)(offset_part, all_fields[own_length, own_cross], all_fields[other_length, other_cross], alive_points[own_length, own_cross], alive_points[other_length, other_cross], same_part, live_part)
        return ((carried[0].at[own_length, own_cross].add(mass_part), carried[1].at[own_length, own_cross].add(spread_part)), None)
    empty_rows = jnp.zeros((length_blocks, cross_count, points), jnp.float32)
    (weighted_volume, spread), _ = lax.scan(first_pass, (empty_rows, empty_rows), packed)
    inverse_volume = 1.0 / jnp.maximum(weighted_volume, 1.0)
    state_rows = jnp.stack([3.0 * spread * inverse_volume, inverse_volume], axis=2)

    def second_pass(carried, scan_item):
        own_length, own_cross, other_length, other_cross, same_part, live_part, offset_part = scan_item

        def tile_second(offset, fields_first, fields_second, alive_first, alive_second, same_block, pair_flag, state_first, state_second):
            valid_bonds, self_bonds = tile_valid(alive_first, alive_second, same_block, pair_flag)
            return second_terms(lattice_points, offset, fields_first, fields_second, valid_bonds, self_bonds, state_first, state_second)
        force_part = jax.vmap(tile_second)(offset_part, all_fields[own_length, own_cross], all_fields[other_length, other_cross], alive_points[own_length, own_cross], alive_points[other_length, other_cross], same_part, live_part, state_rows[own_length, own_cross], state_rows[other_length, other_cross])
        return (carried.at[own_length, own_cross].add(force_part), None)
    force_sums, _ = lax.scan(second_pass, jnp.zeros((length_blocks, cross_count, 3, points), jnp.float32), packed)
    return (force_sums + body_force) * alive_points[:, :, None, :]
```

```python
import jax
import jax.numpy as jnp
from jax import lax
from jax.experimental import pallas as pl
from jax.experimental.pallas import tpu as pltpu
from jax.sharding import PartitionSpec as P

F32 = jnp.float32
AXES = ("gx", "yz")
BLOCKS = 3
ROWS = 24
TILES = 3
LANE0 = 32
HALO = 3
WIDE = 16
FIELDS = 8
TINY = 1e-12


def classes():
    def near(i):
        return i // 3 - 1, lax.rem(i, 3) - 1

    def middle(i):
        j = i - 10
        first = i < 10
        dy = jnp.where(first, (i // 5) * 4 - 2, lax.div(jnp.maximum(j, 0), 2) - 1)
        dz = jnp.where(first, lax.rem(i, 5) - 2, lax.rem(jnp.maximum(j, 0), 2) * 4 - 2)
        return dy, dz

    def far(i):
        j = jnp.maximum(i - 6, 0)
        first = i < 6
        dy = jnp.where(first, (i // 3) * 6 - 3, lax.rem(j, 3) - 1)
        dz = jnp.where(first, lax.rem(i, 3) - 1, (j // 3) * 6 - 3)
        return dy, dz

    return ((9, near, 3), (16, middle, 2), (12, far, 1))


def pack_kernel(counts, jitter, displacement, volume, phase, own, low, high):
    column = lax.axis_index("gx")
    first = lax.axis_index("yz") * BLOCKS
    position = lax.broadcasted_iota(jnp.int32, (1, 512), 1)
    for b in range(BLOCKS):
        alive = position < counts[column, first + b]
        outs = [own.at[b]]
        if b == 0:
            outs.append(low.at[0])
        if b == BLOCKS - 1:
            outs.append(high.at[0])
        for out in outs:
            out[0:3, :] = jitter[b]
            out[3:6, :] = displacement[b]
            out[6:7, :] = jnp.where(alive, volume[b : b + 1, :], 0.0)
            out[7:8, :] = phase[b : b + 1, :].astype(F32)


def place(block_of, fields, base):
    lane = lax.broadcasted_iota(jnp.int32, (8, 128), 1)
    low_half = lane < 64
    zero = jnp.zeros((8, 128), F32)
    for pair in range(4):
        for tile in range(TILES):
            a = block_of(2 * tile, pair)
            b = block_of(2 * tile + 1, pair) if 2 * tile + 1 < 5 else zero
            even = jnp.where(low_half, a, pltpu.roll(b, 64, 1))
            odd = jnp.where(low_half, pltpu.roll(a, 64, 1), b)
            for k, value in enumerate((even, odd)):
                row = tile * ROWS + base + 2 * pair + k
                fields[pl.ds(row, 8, stride=TILES * ROWS), :] = value


def force_kernel(
    counts,
    own,
    chip,
    far,
    body_force,
    residual,
    fields,
    windows,
    bonds,
    state,
):
    column = lax.axis_index("gx")
    first = lax.axis_index("yz") * BLOCKS
    odd = lax.rem(column, 2)
    chip_base = jnp.where(odd == 0, 16, 0)
    far_base = 16 - chip_base
    other = 1 - odd

    def cut(ref, b, pair):
        return ref[b, :, pl.ds(128 * pair, 128)]

    place(lambda b, p: cut(own, b, p), fields, 8)
    place(lambda b, p: chip[pl.ds(other, 1), b, :, pl.ds(128 * p, 128)][0], fields, chip_base)
    place(lambda b, p: cut(far, b, p), fields, far_base)

    rows_lanes = (TILES * ROWS, 128)
    row = lax.broadcasted_iota(jnp.int32, rows_lanes, 0)
    lane72 = lax.broadcasted_iota(jnp.int32, rows_lanes, 1)
    tile_of = row // ROWS
    lattice = (
        (lax.rem(row, ROWS) - 8).astype(F32),
        (tile_of * 16 + lane72 // 8 - 8).astype(F32),
        lax.rem(lane72, 8).astype(F32),
    )
    span = TILES * ROWS

    def field(f):
        return pl.ds(f * span, span)

    for c in range(3):
        reference = fields[field(c), :] + lattice[c]
        fields[field(c), :] = reference
        fields[field(3 + c), :] = reference + fields[field(3 + c), :]

    lane = lax.broadcasted_iota(jnp.int32, (ROWS, 128), 1)
    z_of = lax.rem(lane, 8)

    def build(slot, dy, dz):
        shift = LANE0 + dy * 8 + dz
        back = 128 - shift
        same = lane < back
        inside = (z_of + dz >= 0) & (z_of + dz < 8)
        for f in range(FIELDS):
            turned = [
                pltpu.roll(fields[pl.ds(f * span + t * ROWS, ROWS), :], back, 1)
                for t in range(TILES)
            ]
            for t in range(2):
                value = jnp.where(same, turned[t], turned[t + 1])
                if f == 6:
                    value = jnp.where(inside, value, 0.0)
                windows[slot, f, t] = value

    groups = classes()
    slot0, bond0, starts = 0, 0, []
    for count, where, reach in groups:
        starts.append((slot0, bond0))

        def fill(i, carry, slot0=slot0, where=where):
            dy, dz = where(i)
            build(slot0 + i, dy, dz)
            return carry

        lax.fori_loop(0, count, fill, 0)
        slot0 += count
        bond0 += count * (2 * reach + 1)

    centre = 4
    patches = [(t, h) for t in range(2) for h in range(WIDE // 8)]

    def rows_at(h, dx):
        return pl.ds(8 - HALO + 8 * h + dx, 8)

    points = {
        (t, h): [windows[centre, f, t, rows_at(h, 0), :] for f in (0, 1, 2, 3, 4, 5, 7)]
        for t, h in patches
    }
    zero = jnp.zeros((8, 128), F32)
    sums = tuple(zero for _ in range(2 * len(patches)))
    for (count, where, reach), (slot0, bond0) in zip(groups, starts):
        width = 2 * reach + 1

        def first_pass(i, sums, slot0=slot0, bond0=bond0, reach=reach, width=width):
            sums = list(sums)
            slot = slot0 + i
            bond = bond0 + i * width
            apart = jnp.where(slot == centre, 0.0, 1.0)
            for n, (t, h) in enumerate(patches):
                p = points[t, h]
                for dx in range(-reach, reach + 1):
                    q = [windows[slot, f, t, rows_at(h, dx), :] for f in range(FIELDS)]
                    d = [q[c] - p[c] for c in range(6)]
                    r2 = d[0] * d[0] + d[1] * d[1] + d[2] * d[2]
                    l2 = d[3] * d[3] + d[4] * d[4] + d[5] * d[5]
                    volume = jnp.where(q[7] == p[6], q[6], 0.0)
                    if dx == 0 and reach == 3:
                        r2 = jnp.maximum(r2, TINY)
                        l2 = jnp.maximum(l2, TINY)
                        volume = volume * apart
                    over = lax.rsqrt(l2)
                    r = r2 * lax.rsqrt(r2)
                    e = l2 * over - r
                    near = jnp.maximum(1.0 - r * (1.0 / 3.0), 0.0)
                    omega = near * near * volume
                    wr = omega * r
                    sums[2 * n] = sums[2 * n] + wr * r
                    sums[2 * n + 1] = sums[2 * n + 1] + wr * e
                    at = pl.ds(8 * h, 8)
                    bonds[bond + dx + reach, 0, t, at, :] = omega * over
                    bonds[bond + dx + reach, 1, t, at, :] = r
                    bonds[bond + dx + reach, 2, t, at, :] = e
            return tuple(sums)

        sums = lax.fori_loop(0, count, first_pass, sums)

    for n, (t, h) in enumerate(patches):
        kappa = 1.0 / jnp.maximum(sums[2 * n], 1.0)
        theta = 3.0 * sums[2 * n + 1] * kappa
        state[0, t, pl.ds(8 * h, 8), :] = 105.0 * theta * kappa
        state[1, t, pl.ds(8 * h, 8), :] = 225.0 * kappa

    lane16 = lax.broadcasted_iota(jnp.int32, (WIDE, 128), 1)
    own_rows = pl.ds(HALO, 8)
    own_state = [[state[k, t, own_rows, :] for k in range(2)] for t in range(2)]
    own_place = [[windows[centre, 3 + c, t, pl.ds(8, 8), :] for c in range(3)] for t in range(2)]
    totals = tuple(zero for _ in range(6))
    for (count, where, reach), (slot0, bond0) in zip(groups, starts):
        width = 2 * reach + 1

        def second_pass(i, totals, slot0=slot0, bond0=bond0, reach=reach, width=width, where=where):
            totals = list(totals)
            slot = slot0 + i
            bond = bond0 + i * width
            dy, dz = where(i)
            shift = dy * 8 + dz
            back = lax.rem(256 - shift, 128)
            same = (lane16 + shift >= 0) & (lane16 + shift < 128)
            for k in range(2):
                turned = [pltpu.roll(state[k, t], back, 1) for t in range(2)]
                for t in range(2):
                    state[2 + k, t] = jnp.where(same, turned[t], turned[1 - t])
            for t in range(2):
                for dx in range(-reach, reach + 1):
                    there = pl.ds(HALO + dx, 8)
                    lead = own_state[t][0] + state[2, t, there, :]
                    pull = own_state[t][1] + state[3, t, there, :]
                    u = bonds[bond + dx + reach, 0, t, own_rows, :]
                    r = bonds[bond + dx + reach, 1, t, own_rows, :]
                    e = bonds[bond + dx + reach, 2, t, own_rows, :]
                    scaled = u * (r * lead + e * pull)
                    for c in range(3):
                        y = windows[slot, 3 + c, t, pl.ds(8 + dx, 8), :] - own_place[t][c]
                        totals[3 * t + c] = totals[3 * t + c] + scaled * y
            return tuple(totals)

        totals = lax.fori_loop(0, count, second_pass, totals)

    lane8 = lax.broadcasted_iota(jnp.int32, (8, 128), 1)
    position = lax.broadcasted_iota(jnp.int32, (8, 64), 0) * 64 + lax.broadcasted_iota(
        jnp.int32, (8, 64), 1
    )
    for c in range(3):
        left, right = totals[c], totals[3 + c]
        turned = pltpu.roll(left, 96, 1)
        turned_right = pltpu.roll(right, 96, 1)
        joined = jnp.where(lane8 < 96, turned, turned_right)
        for b in range(BLOCKS):
            source = joined if b < 2 else turned_right
            part = source[:, 64 * (b % 2) : 64 * (b % 2) + 64]
            alive = position < counts[column, first + b]
            for x in range(8):
                at = pl.ds(64 * x, 64)
                value = part[x : x + 1, :] + body_force[b, c : c + 1, at]
                residual[b, c : c + 1, at] = jnp.where(alive[x : x + 1, :], value, 0.0)


def pair_swap(values, sources, extent):
    lengths, heights = lax.axis_size("gx"), lax.axis_size("yz")
    table = []
    for g in range(lengths):
        for z in range(heights):
            dg, dz = extent(g, z)
            if 0 <= g + dg < lengths and 0 <= z + dz < heights:
                table.append((g * heights + z, (g + dg) * heights + z + dz))
    return lax.ppermute(values, AXES, table)


def body(jitter, displacement, volume, body_force, phase, counts, pair_list, pair_live):
    vmem = pl.BlockSpec(memory_space=pltpu.VMEM)
    smem = pl.BlockSpec(memory_space=pltpu.SMEM)
    points = volume.shape[-1]
    block = lambda n: jax.ShapeDtypeStruct((n, FIELDS, points), F32)
    own, low, high = pl.pallas_call(
        pack_kernel,
        out_shape=(block(BLOCKS), block(1), block(1)),
        in_specs=[smem] + [vmem] * 4,
        out_specs=(vmem,) * 3,
    )(counts, jitter[0], displacement[0], volume[0], phase[0])
    below = pair_swap(high, None, lambda g, z: (0, 1))
    above = pair_swap(low, None, lambda g, z: (0, -1))
    own5 = jnp.concatenate([below, own, above], axis=0)
    far = pair_swap(own5, None, lambda g, z: (1 if g % 2 else -1, 0))
    lengths, heights = lax.axis_size("gx"), lax.axis_size("yz")
    chips = [[g * heights + z, (g + 1) * heights + z] for g in range(0, lengths, 2) for z in range(heights)]
    chip = lax.all_gather(own5, AXES, axis=0, axis_index_groups=chips)
    bond_total = sum(n * (2 * reach + 1) for n, _, reach in classes())
    slots = sum(n for n, _, _ in classes())
    residual = pl.pallas_call(
        force_kernel,
        out_shape=jax.ShapeDtypeStruct((BLOCKS, 3, points), F32),
        in_specs=[smem] + [vmem] * 4,
        out_specs=vmem,
        scratch_shapes=[
            pltpu.VMEM((FIELDS * TILES * ROWS, 128), F32),
            pltpu.VMEM((slots, FIELDS, 2, ROWS, 128), F32),
            pltpu.VMEM((bond_total, 3, 2, WIDE, 128), F32),
            pltpu.VMEM((4, 2, WIDE, 128), F32),
        ],
        compiler_params=pltpu.CompilerParams(vmem_limit_bytes=40 * 1024 * 1024),
    )(counts, own5, chip, far, body_force[0])
    return residual[None]


def solution(mesh):
    return jax.shard_map(
        body,
        mesh=mesh,
        in_specs=(
            P("gx", "yz", None, None),
            P("gx", "yz", None, None),
            P("gx", "yz", None),
            P("gx", "yz", None, None),
            P("gx", "yz", None),
            P(),
            P(("gx", "yz"), None),
            P(("gx", "yz")),
        ),
        out_specs=P("gx", "yz", None, None),
        check_vma=False,
    )
```

```python
import functools

import jax
import jax.numpy as jnp
from jax import lax
from jax.experimental import pallas as pl
from jax.experimental.pallas import tpu as pltpu
from jax.sharding import PartitionSpec as P

F32 = jnp.float32
AXES = ("gx", "yz")
BLOCKS = 3
ROWS = 24
TILES = 3
LANE0 = 32
HALO = 3
WIDE = 16
FIELDS = 8
HORIZON = 3.0


CLASSES = ((8, 3), (16, 2), (12, 1))
CENTRE = sum(count for count, _ in CLASSES)
BONDS = sum(count * (2 * reach + 1) for count, reach in CLASSES)


def shift_of(slot):
    if isinstance(slot, int):
        near = [(y, z) for y in (-1, 0, 1) for z in (-1, 0, 1) if (y, z) != (0, 0)]
        middle = [(y, z) for y in (-2, 2) for z in range(-2, 3)]
        middle += [(y, z) for y in (-1, 0, 1) for z in (-2, 2)]
        far = [(y, z) for y in (-3, 3) for z in (-1, 0, 1)]
        far += [(y, z) for z in (-3, 3) for y in (-1, 0, 1)]
        return (near + middle + far + [(0, 0)])[slot]
    i = slot + (slot >= 4).astype(jnp.int32)
    near = (lax.div(i, 3) - 1, lax.rem(i, 3) - 1)
    i = jnp.maximum(slot - 8, 0)
    j = jnp.maximum(i - 10, 0)
    wide = i < 10
    middle = (
        jnp.where(wide, lax.div(i, 5) * 4 - 2, lax.div(j, 2) - 1),
        jnp.where(wide, lax.rem(i, 5) - 2, lax.rem(j, 2) * 4 - 2),
    )
    i = jnp.maximum(slot - 24, 0)
    j = jnp.maximum(i - 6, 0)
    wide = i < 6
    far = (
        jnp.where(wide, lax.div(i, 3) * 6 - 3, lax.rem(j, 3) - 1),
        jnp.where(wide, lax.rem(i, 3) - 1, lax.div(j, 3) * 6 - 3),
    )
    return tuple(
        jnp.where(slot < 8, n, jnp.where(slot < 24, m, jnp.where(slot < 36, f, 0)))
        for n, m, f in zip(near, middle, far)
    )


def pack_kernel(
    counts,
    jitter,
    displacement,
    volume,
    phase,
    own,
    edge_odd,
    edge_even,
    count_row,
    jitters,
    displacements,
    volumes,
    phases,
    arrived,
):
    column = lax.axis_index("gx")
    place_z = lax.axis_index("yz")
    copies = [
        pltpu.make_async_copy(source, target, arrived.at[n])
        for n, (source, target) in enumerate(
            (
                (jitter, jitters),
                (displacement, displacements),
                (volume, volumes),
                (phase, phases),
                (counts.at[pl.ds(column // 8 * 8, 8)], count_row),
            )
        )
    ]
    for copy in copies:
        copy.start()
    for copy in copies:
        copy.wait()
    position = lax.broadcasted_iota(jnp.int32, (1, 512), 1)
    for b in range(BLOCKS):
        alive = position < count_row[lax.rem(column, 8), place_z * BLOCKS + b]
        for c in range(3):
            own[b, c : c + 1, :] = jitters[b, c]
            own[b, 3 + c : 4 + c, :] = displacements[b, c]
        own[b, 6:7, :] = jnp.where(alive, volumes[b], 0.0)
        own[b, 7:8, :] = phases[b].astype(F32)
    odd = lax.rem(place_z, 2) == 1
    first, last = own[0], own[BLOCKS - 1]
    edge_odd[0] = jnp.where(odd, last, first)
    edge_even[0] = jnp.where(odd, first, last)


def place(block_of, fields, base):
    lane = lax.broadcasted_iota(jnp.int32, (8, 128), 1)
    low_half = lane < 64
    zero = jnp.zeros((8, 128), F32)
    for pair in range(4):
        for tile in range(TILES):
            a = block_of(2 * tile, pair)
            b = block_of(2 * tile + 1, pair) if 2 * tile + 1 < 5 else zero
            even = jnp.where(low_half, a, pltpu.roll(b, 64, 1))
            odd = jnp.where(low_half, pltpu.roll(a, 64, 1), b)
            for k, value in enumerate((even, odd)):
                row = tile * ROWS + base + 2 * pair + k
                fields[pl.ds(row, 8, stride=TILES * ROWS), :] = value


def force_kernel(
    extents,
    counts,
    own,
    chip,
    far,
    body_force,
    residual,
    fields,
    window_a,
    window_b,
    points,
    places,
    bonds,
    state,
    states,
):
    column = lax.axis_index("gx")
    first = lax.axis_index("yz") * BLOCKS
    odd = lax.rem(column, 2)
    chip_base = jnp.where(odd == 0, 16, 0)
    far_base = 16 - chip_base
    other = 1 - odd

    flip = 4 * lax.rem(lax.axis_index("yz"), 2)
    order = (flip, 1, 2, 3, 4 - flip)

    def lanes(pair):
        return pl.ds(128 * pair, 128)

    place(lambda b, p: own[pl.ds(order[b], 1), :, lanes(p)][0], fields, 8)
    place(lambda b, p: chip[pl.ds(other * 5 + order[b], 1), :, lanes(p)][0], fields, chip_base)
    place(lambda b, p: far[pl.ds(order[b], 1), :, lanes(p)][0], fields, far_base)

    span = TILES * ROWS
    row = lax.broadcasted_iota(jnp.int32, (span, 128), 0)
    lane72 = lax.broadcasted_iota(jnp.int32, (span, 128), 1)
    lattice = (
        (lax.rem(row, ROWS) - 8).astype(F32),
        (lax.div(row, ROWS) * 16 + lax.div(lane72, 8) - 8).astype(F32),
        lax.rem(lane72, 8).astype(F32),
    )

    def field(f):
        return pl.ds(f * span, span)

    for c in range(3):
        reference = fields[field(c), :] + lattice[c]
        if c == 2:
            reference = reference + 8.0 * fields[field(7), :]
        current = reference + fields[field(3 + c), :]
        fields[field(c), :] = reference * (1.0 / HORIZON)
        fields[field(3 + c), :] = current * (1.0 / HORIZON)
    along = column * 8 + lax.rem(row, ROWS) - 8
    across = first * 8 + lax.div(row, ROWS) * 16 + lax.div(lane72, 8) - 8
    inner = (along >= 0) & (along < extents[0] * 8) & (across >= 0) & (across < extents[1] * 8)
    fields[field(6), :] = jnp.where(inner, fields[field(6), :], 0.0)

    lane = lax.broadcasted_iota(jnp.int32, (8, 128), 1)
    z_of = lax.rem(lane, 8)

    def build(window, slot):
        dy, dz = shift_of(slot)
        back = 128 - (LANE0 + dy * 8 + dz)
        same = lane < back
        inside = (z_of + dz >= 0) & (z_of + dz < 8)

        def step(f, h):
            at = pl.ds(8 * h, 8)
            turned = [
                pltpu.roll(fields[pl.ds(f * span + t * ROWS + 8 * h, 8), :], back, 1)
                for t in range(TILES)
            ]
            for t in range(2):
                value = jnp.where(same, turned[t], turned[t + 1])
                if f == 6:
                    value = jnp.where(inside, value, 0.0)
                window[f, t, at, :] = value
                if 3 <= f < 6:
                    places[slot, f - 3, t, at, :] = value

        return [functools.partial(step, f, h) for f in range(7) for h in range(ROWS // 8)]

    def run(steps):
        for step in steps:
            step()

    patches = [(t, h) for t in range(2) for h in range(WIDE // 8)]

    def bond_sums(window, reach, bond, sums, beside=(), skip=None):
        sums = list(sums)
        total = len(patches) * (2 * reach + 1)
        done, placed = 0, 0
        for n, (t, h) in enumerate(patches):
            p = [points[c, t, pl.ds(8 * h, 8), :] for c in range(6)]
            for dx in range(-reach, reach + 1):
                done += 1
                while placed * total < done * len(beside):
                    beside[placed]()
                    placed += 1
                if dx == skip:
                    continue
                there = pl.ds(8 - HALO + 8 * h + dx, 8)
                d = [window[c, t, there, :] - p[c] for c in range(6)]
                r2 = d[0] * d[0] + d[1] * d[1] + d[2] * d[2]
                l2 = d[3] * d[3] + d[4] * d[4] + d[5] * d[5]
                over = lax.rsqrt(l2)
                r = r2 * lax.rsqrt(r2)
                e = l2 * over - r
                near = jnp.maximum(1.0 - r, 0.0)
                omega = near * near * window[6, t, there, :]
                wr = omega * r
                sums[2 * n] = sums[2 * n] + wr * r
                sums[2 * n + 1] = sums[2 * n + 1] + wr * e
                at = pl.ds(8 * h, 8)
                bonds[bond + dx + reach, 0, t, at, :] = omega * over
                bonds[bond + dx + reach, 1, t, at, :] = r
                bonds[bond + dx + reach, 2, t, at, :] = e
        return tuple(sums)

    run(build(window_b, CENTRE))
    for t in range(2):
        for c in range(6):
            points[c, t] = window_b[c, t, pl.ds(8 - HALO, WIDE), :]
    zero = jnp.zeros((8, 128), F32)
    sums = tuple(zero for _ in range(2 * len(patches)))
    sums = bond_sums(window_b, 3, BONDS, sums, build(window_a, 0), skip=0)
    slot0, bond0 = 0, 0
    for count, reach in CLASSES:
        width = 2 * reach + 1

        def first_pass(k, sums, slot0=slot0, bond0=bond0, reach=reach, width=width):
            slot = slot0 + 2 * k
            bond = bond0 + 2 * k * width
            sums = bond_sums(window_a, reach, bond, sums, build(window_b, slot + 1))
            return bond_sums(window_b, reach, bond + width, sums, build(window_a, slot + 2))

        sums = lax.fori_loop(0, count // 2, first_pass, sums)
        slot0 += count
        bond0 += count * width

    for n, (t, h) in enumerate(patches):
        scale = HORIZON * HORIZON
        kappa = 1.0 / jnp.maximum(scale * sums[2 * n], 1.0)
        theta = 3.0 * scale * sums[2 * n + 1] * kappa
        state[0, t, pl.ds(8 * h, 8), :] = 105.0 * HORIZON * theta * kappa
        state[1, t, pl.ds(8 * h, 8), :] = 225.0 * HORIZON * kappa

    lane16 = lax.broadcasted_iota(jnp.int32, (WIDE, 128), 1)
    for slot in range(CENTRE + 1):
        dy, dz = shift_of(slot)
        shift = dy * 8 + dz
        same = (lane16 + shift >= 0) & (lane16 + shift < 128)
        for k in range(2):
            if shift == 0:
                for t in range(2):
                    states[slot, k, t] = state[k, t]
                continue
            turned = [pltpu.roll(state[k, t], -shift % 128, 1) for t in range(2)]
            for t in range(2):
                states[slot, k, t] = jnp.where(same, turned[t], turned[1 - t])

    own_rows = pl.ds(HALO, 8)

    def forces(slot, reach, bond, totals, skip=None):
        totals = list(totals)
        for t in range(2):
            own_state = [state[k, t, own_rows, :] for k in range(2)]
            own_place = [points[3 + c, t, own_rows, :] for c in range(3)]
            for dx in range(-reach, reach + 1):
                if dx == skip:
                    continue
                there = pl.ds(HALO + dx, 8)
                lead = own_state[0] + states[slot, 0, t, there, :]
                pull = own_state[1] + states[slot, 1, t, there, :]
                u, r, e = (bonds[bond + dx + reach, k, t, own_rows, :] for k in range(3))
                scaled = u * (r * lead + e * pull)
                for c in range(3):
                    y = places[slot, c, t, pl.ds(8 + dx, 8), :] - own_place[c]
                    totals[3 * t + c] = totals[3 * t + c] + scaled * y
        return tuple(totals)

    totals = forces(CENTRE, 3, BONDS, tuple(zero for _ in range(6)), skip=0)
    slot0, bond0 = 0, 0
    for count, reach in CLASSES:
        width = 2 * reach + 1

        def second_pass(k, totals, slot0=slot0, bond0=bond0, reach=reach, width=width):
            for i in range(2):
                totals = forces(slot0 + 2 * k + i, reach, bond0 + (2 * k + i) * width, totals)
            return totals

        totals = lax.fori_loop(0, count // 2, second_pass, totals)
        slot0 += count
        bond0 += count * width

    lane8 = lax.broadcasted_iota(jnp.int32, (8, 128), 1)
    position = lax.broadcasted_iota(jnp.int32, (8, 64), 0) * 64 + lax.broadcasted_iota(
        jnp.int32, (8, 64), 1
    )
    for c in range(3):
        left, right = totals[c], totals[3 + c]
        turned = pltpu.roll(left, 96, 1)
        turned_right = pltpu.roll(right, 96, 1)
        joined = jnp.where(lane8 < 96, turned, turned_right)
        for b in range(BLOCKS):
            source = joined if b < 2 else turned_right
            part = source[:, 64 * (b % 2) : 64 * (b % 2) + 64]
            alive = position < counts[column, first + b]
            for x in range(8):
                at = pl.ds(64 * x, 64)
                value = part[x : x + 1, :] + body_force[b, c, :, at]
                residual[b, c, :, at] = jnp.where(alive[x : x + 1, :], value, 0.0)


def permute(values, extent):
    lengths, heights = lax.axis_size("gx"), lax.axis_size("yz")
    table = []
    for g in range(lengths):
        for z in range(heights):
            dg, dz = extent(g, z)
            if 0 <= g + dg < lengths and 0 <= z + dz < heights:
                table.append((g * heights + z, (g + dg) * heights + z + dz))
    return lax.ppermute(values, AXES, table)


def run_force(counts, own5, chip, far, body_force):
    vmem = pl.BlockSpec(memory_space=pltpu.VMEM)
    smem = pl.BlockSpec(memory_space=pltpu.SMEM)
    points = own5.shape[-1]
    return pl.pallas_call(
        functools.partial(force_kernel, counts.shape),
        out_shape=jax.ShapeDtypeStruct((BLOCKS, 3, 1, points), F32),
        in_specs=[smem] + [vmem] * 4,
        out_specs=vmem,
        scratch_shapes=[
            pltpu.VMEM((FIELDS * TILES * ROWS, 128), F32),
            pltpu.VMEM((7, 2, ROWS, 128), F32),
            pltpu.VMEM((7, 2, ROWS, 128), F32),
            pltpu.VMEM((6, 2, WIDE, 128), F32),
            pltpu.VMEM((CENTRE + 1, 3, 2, ROWS, 128), F32),
            pltpu.VMEM((BONDS + 7, 3, 2, WIDE, 128), F32),
            pltpu.VMEM((2, 2, WIDE, 128), F32),
            pltpu.VMEM((CENTRE + 1, 2, 2, WIDE, 128), F32),
        ],
        compiler_params=pltpu.CompilerParams(vmem_limit_bytes=24 * 1024 * 1024),
    )(counts, own5, chip, far, body_force)


def flat(values):
    return jnp.moveaxis(values, 0, -2)


def body(jitter, displacement, volume, body_force, phase, counts, pair_list, pair_live):
    vmem = pl.BlockSpec(memory_space=pltpu.VMEM)
    points = volume.shape[-1]
    block = lambda n: jax.ShapeDtypeStruct((n, FIELDS, points), F32)
    own, edge_odd, edge_even = pl.pallas_call(
        pack_kernel,
        out_shape=(block(BLOCKS), block(1), block(1)),
        in_specs=[pl.BlockSpec(memory_space=pltpu.HBM)] * 5,
        out_specs=(vmem,) * 3,
        scratch_shapes=[
            pltpu.SMEM((8, counts.shape[1]), jnp.int32),
            pltpu.VMEM((BLOCKS, 3, 1, points), F32),
            pltpu.VMEM((BLOCKS, 3, 1, points), F32),
            pltpu.VMEM((BLOCKS, 1, points), F32),
            pltpu.VMEM((BLOCKS, 1, points), jnp.int32),
            pltpu.SemaphoreType.DMA((5,)),
        ],
        compiler_params=pltpu.CompilerParams(vmem_limit_bytes=60 * 1024 * 1024),
    )(counts, flat(jitter), flat(displacement), flat(volume), flat(phase))
    lengths, heights = lax.axis_size("gx"), lax.axis_size("yz")

    def device(g, z):
        return g * heights + z

    def pairs(couples):
        return [[device(*a), device(*b)] for a, b in couples]

    from_even = permute(edge_even, lambda g, z: (0, -1 if z % 2 else 1))
    couples = [((g, z), (g, z + 1)) for g in range(lengths) for z in range(1, heights - 1, 2)]
    couples += [((g, z), (g + 1, z)) for g in range(0, lengths, 2) for z in (0, heights - 1)]
    ends = lax.all_gather(edge_odd, AXES, axis=0, tiled=True, axis_index_groups=pairs(couples))
    odd = lax.rem(lax.axis_index("yz"), 2) == 1
    from_odd = jnp.where(odd, ends[1:], ends[:1])
    own5 = jnp.concatenate([from_odd, own, from_even], axis=0)
    far = permute(own5, lambda g, z: (1 if g % 2 else -1, 0))
    couples = [((g, z), (g + 1, z)) for g in range(0, lengths, 2) for z in range(heights)]
    chip = lax.all_gather(own5, AXES, axis=0, tiled=True, axis_index_groups=pairs(couples))
    residual = run_force(counts, own5, chip, far, flat(body_force))
    return jnp.moveaxis(residual, 2, 0)


def solution(mesh):
    return jax.shard_map(
        body,
        mesh=mesh,
        in_specs=(
            P("gx", "yz", None, None),
            P("gx", "yz", None, None),
            P("gx", "yz", None),
            P("gx", "yz", None, None),
            P("gx", "yz", None),
            P(),
            P(("gx", "yz"), None),
            P(("gx", "yz")),
        ),
        out_specs=P("gx", "yz", None, None),
        check_vma=False,
    )
```

```python
import functools

import jax
import jax.numpy as jnp
from jax import lax
from jax.experimental import pallas as pl
from jax.experimental.pallas import tpu as pltpu
from jax.sharding import PartitionSpec as P

F32 = jnp.float32
AXES = ("gx", "yz")
BLOCKS = 3
ROWS = 24
TILES = 3
LANE0 = 32
HALO = 3
WIDE = 16
FIELDS = 8
HORIZON = 3.0


REACHES = (3,) * 8 + (2,) * 16 + (1,) * 12 + (3,)
CENTRE = len(REACHES) - 1
BONDS = sum(2 * reach + 1 for reach in REACHES)


def shifts():
    near = [(y, z) for y in (-1, 0, 1) for z in (-1, 0, 1) if (y, z) != (0, 0)]
    middle = [(y, z) for y in (-2, 2) for z in range(-2, 3)]
    middle += [(y, z) for y in (-1, 0, 1) for z in (-2, 2)]
    far = [(y, z) for y in (-3, 3) for z in (-1, 0, 1)]
    far += [(y, z) for z in (-3, 3) for y in (-1, 0, 1)]
    return near + middle + far + [(0, 0)]


SHIFTS = shifts()


def pack_kernel(
    counts,
    jitter,
    displacement,
    volume,
    phase,
    own,
    edge_odd,
    edge_even,
    count_row,
    jitters,
    displacements,
    volumes,
    phases,
    arrived,
):
    column = lax.axis_index("gx")
    place_z = lax.axis_index("yz")
    copies = [
        pltpu.make_async_copy(source, target, arrived.at[n])
        for n, (source, target) in enumerate(
            (
                (jitter, jitters),
                (displacement, displacements),
                (volume, volumes),
                (phase, phases),
                (counts.at[pl.ds(column // 8 * 8, 8)], count_row),
            )
        )
    ]
    for copy in copies:
        copy.start()
    for copy in copies:
        copy.wait()
    position = lax.broadcasted_iota(jnp.int32, (1, 512), 1)
    for b in range(BLOCKS):
        alive = position < count_row[lax.rem(column, 8), place_z * BLOCKS + b]
        for c in range(3):
            own[b, c : c + 1, :] = jitters[b, c]
            own[b, 3 + c : 4 + c, :] = displacements[b, c]
        own[b, 6:7, :] = jnp.where(alive, volumes[b], 0.0)
        own[b, 7:8, :] = phases[b].astype(F32)
    odd = lax.rem(place_z, 2) == 1
    first, last = own[0], own[BLOCKS - 1]
    edge_odd[0] = jnp.where(odd, last, first)
    edge_even[0] = jnp.where(odd, first, last)


def place(block_of, fields, base):
    lane = lax.broadcasted_iota(jnp.int32, (8, 128), 1)
    low_half = lane < 64
    zero = jnp.zeros((8, 128), F32)
    for pair in range(4):
        for tile in range(TILES):
            a = block_of(2 * tile, pair)
            b = block_of(2 * tile + 1, pair) if 2 * tile + 1 < 5 else zero
            even = jnp.where(low_half, a, pltpu.roll(b, 64, 1))
            odd = jnp.where(low_half, pltpu.roll(a, 64, 1), b)
            for k, value in enumerate((even, odd)):
                row = tile * ROWS + base + 2 * pair + k
                fields[pl.ds(row, 8, stride=TILES * ROWS), :] = value


def force_kernel(
    extents,
    own,
    chip,
    far,
    body_force,
    residual,
    fields,
    windows,
    bonds,
    state,
    states,
    turn,
):
    column = lax.axis_index("gx")
    first = lax.axis_index("yz") * BLOCKS
    odd = lax.rem(column, 2)
    chip_base = jnp.where(odd == 0, 16, 0)
    far_base = 16 - chip_base
    other = 1 - odd

    flip = 4 * lax.rem(lax.axis_index("yz"), 2)
    stack = (flip, 1, 2, 3, 4 - flip)

    def lanes(pair):
        return pl.ds(128 * pair, 128)

    place(lambda b, p: own[pl.ds(stack[b], 1), :, lanes(p)][0], fields, 8)
    place(lambda b, p: chip[pl.ds(other * 5 + stack[b], 1), :, lanes(p)][0], fields, chip_base)
    place(lambda b, p: far[pl.ds(stack[b], 1), :, lanes(p)][0], fields, far_base)

    span = TILES * ROWS
    row = lax.broadcasted_iota(jnp.int32, (span, 128), 0)
    lane72 = lax.broadcasted_iota(jnp.int32, (span, 128), 1)
    lattice = (
        (lax.rem(row, ROWS) - 8).astype(F32),
        (lax.div(row, ROWS) * 16 + lax.div(lane72, 8) - 8).astype(F32),
        lax.rem(lane72, 8).astype(F32),
    )

    def field(f):
        return pl.ds(f * span, span)

    for c in range(3):
        reference = fields[field(c), :] + lattice[c]
        if c == 2:
            reference = reference + 8.0 * fields[field(7), :]
        current = reference + fields[field(3 + c), :]
        fields[field(c), :] = reference * (1.0 / HORIZON)
        fields[field(3 + c), :] = current * (1.0 / HORIZON)
    along = column * 8 + lax.rem(row, ROWS) - 8
    across = first * 8 + lax.div(row, ROWS) * 16 + lax.div(lane72, 8) - 8
    inner = (along >= 0) & (along < extents[0] * 8) & (across >= 0) & (across < extents[1] * 8)
    fields[field(6), :] = jnp.where(inner, fields[field(6), :], 0.0)

    lane = lax.broadcasted_iota(jnp.int32, (8, 128), 1)
    z_of = lax.rem(lane, 8)

    def build(slot):
        dy, dz = SHIFTS[slot]
        back = 128 - (LANE0 + dy * 8 + dz)
        same = lane < back
        inside = (z_of + dz >= 0) & (z_of + dz < 8)

        def step(f, h):
            turned = [
                pltpu.roll(fields[pl.ds(f * span + t * ROWS + 8 * h, 8), :], back, 1)
                for t in range(TILES)
            ]
            for t in range(2):
                value = jnp.where(same, turned[t], turned[t + 1])
                if f == 6 and dz != 0:
                    value = jnp.where(inside, value, 0.0)
                windows[slot, f, t, pl.ds(8 * h, 8), :] = value

        return [functools.partial(step, f, h) for f in range(7) for h in range(ROWS // 8)]

    def spread(steps, part, parts):
        for step in steps[len(steps) * part // parts : len(steps) * (part + 1) // parts]:
            step()

    patches = [(t, h) for t in range(2) for h in range(WIDE // 8)]
    starts, bond0 = [], 0
    for reach in REACHES:
        starts.append(bond0)
        bond0 += 2 * reach + 1

    def bond_sums(slot, sums, beside):
        reach, bond = REACHES[slot], starts[slot]
        parts = len(patches) * (2 * reach + 1)
        part = 0
        for n, (t, h) in enumerate(patches):
            at = pl.ds(8 * h, 8)
            p = [windows[CENTRE, c, t, pl.ds(8 - HALO + 8 * h, 8), :] for c in range(6)]
            for dx in range(-reach, reach + 1):
                spread(beside, part, parts)
                part += 1
                if dx == 0 and slot == CENTRE:
                    continue
                there = pl.ds(8 - HALO + 8 * h + dx, 8)
                d = [windows[slot, c, t, there, :] - p[c] for c in range(6)]
                r2 = d[0] * d[0] + d[1] * d[1] + d[2] * d[2]
                l2 = d[3] * d[3] + d[4] * d[4] + d[5] * d[5]
                over = lax.rsqrt(l2)
                r = r2 * lax.rsqrt(r2)
                length = l2 * over
                near = jnp.maximum(1.0 - r, 0.0)
                omega = near * near * windows[slot, 6, t, there, :]
                wr = omega * r
                sums[2 * n] = sums[2 * n] + wr * r
                sums[2 * n + 1] = sums[2 * n + 1] + wr * length
                bonds[bond + dx + reach, 0, t, at, :] = omega * over
                bonds[bond + dx + reach, 1, t, at, :] = r
                bonds[bond + dx + reach, 2, t, at, :] = length

    zero = jnp.zeros((8, 128), F32)
    sums = [zero for _ in range(2 * len(patches))]
    order = [CENTRE] + list(range(CENTRE))
    spread(build(CENTRE), 0, 1)
    for slot, following in zip(order, order[1:] + [None]):
        bond_sums(slot, sums, [] if following is None else build(following))

    for n, (t, h) in enumerate(patches):
        scale = HORIZON * HORIZON
        kappa = 1.0 / jnp.maximum(scale * sums[2 * n], 1.0)
        theta = 3.0 * scale * (sums[2 * n + 1] - sums[2 * n]) * kappa
        pull = 225.0 * HORIZON * kappa
        state[0, t, pl.ds(8 * h, 8), :] = 105.0 * HORIZON * theta * kappa - pull
        state[1, t, pl.ds(8 * h, 8), :] = pull

    lane16 = lax.broadcasted_iota(jnp.int32, (WIDE, 128), 1)

    def build_state(slot):
        dy, dz = SHIFTS[slot]
        shift = dy * 8 + dz
        same = (lane16 + shift >= 0) & (lane16 + shift < 128)

        def step(k):
            turned = [pltpu.roll(state[k, t], -shift % 128, 1) for t in range(2)]
            for t in range(2):
                states[slot, k, t] = jnp.where(same, turned[t], turned[1 - t])

        return [functools.partial(step, k) for k in range(2)]

    own_rows = pl.ds(HALO, 8)

    def forces(slot, totals, beside):
        reach, bond = REACHES[slot], starts[slot]
        for t in range(2):
            spread(beside, t, 2)
            own_state = [state[k, t, own_rows, :] for k in range(2)]
            own_place = [windows[CENTRE, 3 + c, t, pl.ds(8, 8), :] for c in range(3)]
            for dx in range(-reach, reach + 1):
                if dx == 0 and slot == CENTRE:
                    continue
                there = pl.ds(HALO + dx, 8)
                theirs = [
                    (state[k, t, there, :] if slot == CENTRE else states[slot, k, t, there, :])
                    for k in range(2)
                ]
                u, r, length = (bonds[bond + dx + reach, k, t, own_rows, :] for k in range(3))
                scaled = u * (
                    r * (own_state[0] + theirs[0]) + length * (own_state[1] + theirs[1])
                )
                for c in range(3):
                    y = windows[slot, 3 + c, t, pl.ds(8 + dx, 8), :] - own_place[c]
                    totals[3 * t + c] = totals[3 * t + c] + scaled * y

    totals = [zero for _ in range(6)]
    for slot, following in zip(order, order[1:] + [None]):
        forces(slot, totals, [] if following is None else build_state(following))

    lane8 = lax.broadcasted_iota(jnp.int32, (8, 128), 1)
    low_half = lax.broadcasted_iota(jnp.int32, (4, 128), 1) < 64
    for c in range(3):
        left, right = (pltpu.roll(totals[3 * t + c], 96, 1) for t in range(2))
        for n, source in enumerate((jnp.where(lane8 < 96, left, right), right)):
            turn[0] = source
            turn[1] = pltpu.roll(source, 64, 1)
            even, odd_row = pl.ds(0, 4, stride=2), pl.ds(1, 4, stride=2)
            for half in range(2 - n):
                b = 2 * n + half
                part = jnp.where(low_half, turn[half, even, :], turn[1 - half, odd_row, :])
                for pair in range(4):
                    at = lanes(pair)
                    value = part[pair : pair + 1, :] + body_force[b, c, :, at]
                    alive = own[1 + b, 6:7, at] > 0.0
                    residual[b, c, :, at] = jnp.where(alive, value, 0.0)


def permute(values, extent):
    lengths, heights = lax.axis_size("gx"), lax.axis_size("yz")
    table = []
    for g in range(lengths):
        for z in range(heights):
            dg, dz = extent(g, z)
            if 0 <= g + dg < lengths and 0 <= z + dz < heights:
                table.append((g * heights + z, (g + dg) * heights + z + dz))
    return lax.ppermute(values, AXES, table)


def run_force(extents, own5, chip, far, body_force):
    vmem = pl.BlockSpec(memory_space=pltpu.VMEM)
    points = own5.shape[-1]
    return pl.pallas_call(
        functools.partial(force_kernel, extents),
        out_shape=jax.ShapeDtypeStruct((BLOCKS, 3, 1, points), F32),
        in_specs=[vmem] * 4,
        out_specs=vmem,
        scratch_shapes=[
            pltpu.VMEM((FIELDS * TILES * ROWS, 128), F32),
            pltpu.VMEM((CENTRE + 1, 7, 2, ROWS, 128), F32),
            pltpu.VMEM((BONDS, 3, 2, WIDE, 128), F32),
            pltpu.VMEM((2, 2, WIDE, 128), F32),
            pltpu.VMEM((CENTRE, 2, 2, WIDE, 128), F32),
            pltpu.VMEM((2, 8, 128), F32),
        ],
        compiler_params=pltpu.CompilerParams(vmem_limit_bytes=24 * 1024 * 1024),
    )(own5, chip, far, body_force)


def flat(values):
    return jnp.moveaxis(values, 0, -2)


def body(jitter, displacement, volume, body_force, phase, counts, pair_list, pair_live):
    vmem = pl.BlockSpec(memory_space=pltpu.VMEM)
    points = volume.shape[-1]
    block = lambda n: jax.ShapeDtypeStruct((n, FIELDS, points), F32)
    own, edge_odd, edge_even = pl.pallas_call(
        pack_kernel,
        out_shape=(block(BLOCKS), block(1), block(1)),
        in_specs=[pl.BlockSpec(memory_space=pltpu.HBM)] * 5,
        out_specs=(vmem,) * 3,
        scratch_shapes=[
            pltpu.SMEM((8, counts.shape[1]), jnp.int32),
            pltpu.VMEM((BLOCKS, 3, 1, points), F32),
            pltpu.VMEM((BLOCKS, 3, 1, points), F32),
            pltpu.VMEM((BLOCKS, 1, points), F32),
            pltpu.VMEM((BLOCKS, 1, points), jnp.int32),
            pltpu.SemaphoreType.DMA((5,)),
        ],
        compiler_params=pltpu.CompilerParams(vmem_limit_bytes=60 * 1024 * 1024),
    )(counts, flat(jitter), flat(displacement), flat(volume), flat(phase))
    lengths, heights = lax.axis_size("gx"), lax.axis_size("yz")

    def device(g, z):
        return g * heights + z

    def pairs(couples):
        return [[device(*a), device(*b)] for a, b in couples]

    from_even = permute(edge_even, lambda g, z: (0, -1 if z % 2 else 1))
    couples = [((g, z), (g, z + 1)) for g in range(lengths) for z in range(1, heights - 1, 2)]
    couples += [((g, z), (g + 1, z)) for g in range(0, lengths, 2) for z in (0, heights - 1)]
    ends = lax.all_gather(edge_odd, AXES, axis=0, tiled=True, axis_index_groups=pairs(couples))
    odd = lax.rem(lax.axis_index("yz"), 2) == 1
    from_odd = jnp.where(odd, ends[1:], ends[:1])
    own5 = jnp.concatenate([from_odd, own, from_even], axis=0)
    far = permute(own5, lambda g, z: (1 if g % 2 else -1, 0))
    couples = [((g, z), (g + 1, z)) for g in range(0, lengths, 2) for z in range(heights)]
    chip = lax.all_gather(own5, AXES, axis=0, tiled=True, axis_index_groups=pairs(couples))
    residual = run_force(counts.shape, own5, chip, far, flat(body_force))
    return jnp.moveaxis(residual, 2, 0)


def solution(mesh):
    return jax.shard_map(
        body,
        mesh=mesh,
        in_specs=(
            P("gx", "yz", None, None),
            P("gx", "yz", None, None),
            P("gx", "yz", None),
            P("gx", "yz", None, None),
            P("gx", "yz", None),
            P(),
            P(("gx", "yz"), None),
            P(("gx", "yz")),
        ),
        out_specs=P("gx", "yz", None, None),
        check_vma=False,
    )
```

```python
import functools

import jax
import jax.numpy as jnp
from jax import lax
from jax.experimental import pallas as pl
from jax.experimental.pallas import tpu as pltpu
from jax.sharding import PartitionSpec as P

F32 = jnp.float32
AXES = ("gx", "yz")
BLOCKS = 3
ROWS = 24
TILES = 3
LANE0 = 32
HALO = 3
WIDE = 16
FIELDS = 8
HORIZON = 3.0


REACHES = (3,) * 8 + (2,) * 16 + (1,) * 12 + (3,)
CENTRE = len(REACHES) - 1
BONDS = sum(2 * reach + 1 for reach in REACHES)


def shifts():
    near = [(y, z) for y in (-1, 0, 1) for z in (-1, 0, 1) if (y, z) != (0, 0)]
    middle = [(y, z) for y in (-2, 2) for z in range(-2, 3)]
    middle += [(y, z) for y in (-1, 0, 1) for z in (-2, 2)]
    far = [(y, z) for y in (-3, 3) for z in (-1, 0, 1)]
    far += [(y, z) for z in (-3, 3) for y in (-1, 0, 1)]
    return near + middle + far + [(0, 0)]


SHIFTS = shifts()


def pack_kernel(
    counts,
    jitter,
    displacement,
    volume,
    phase,
    own,
    edge_odd,
    edge_even,
    count_row,
    jitters,
    displacements,
    volumes,
    phases,
    arrived,
):
    column = lax.axis_index("gx")
    place_z = lax.axis_index("yz")
    copies = [
        pltpu.make_async_copy(source, target, arrived.at[n])
        for n, (source, target) in enumerate(
            (
                (jitter, jitters),
                (displacement, displacements),
                (volume, volumes),
                (phase, phases),
                (counts.at[pl.ds(column // 8 * 8, 8)], count_row),
            )
        )
    ]
    for copy in copies:
        copy.start()
    for copy in copies:
        copy.wait()
    position = lax.broadcasted_iota(jnp.int32, (1, 512), 1)
    for b in range(BLOCKS):
        alive = position < count_row[lax.rem(column, 8), place_z * BLOCKS + b]
        for c in range(3):
            own[b, c : c + 1, :] = jitters[b, c]
            own[b, 3 + c : 4 + c, :] = displacements[b, c]
        own[b, 6:7, :] = jnp.where(alive, volumes[b], 0.0)
        own[b, 7:8, :] = phases[b].astype(F32)
    odd = lax.rem(place_z, 2) == 1
    first, last = own[0], own[BLOCKS - 1]
    edge_odd[0] = jnp.where(odd, last, first)
    edge_even[0] = jnp.where(odd, first, last)


def place(block_of, fields, base, pairs=4):
    lane = lax.broadcasted_iota(jnp.int32, (8, 128), 1)
    low_half = lane < 64
    zero = jnp.zeros((8, 128), F32)
    for pair in range(pairs):
        for tile in range(TILES):
            a = block_of(2 * tile, pair)
            b = block_of(2 * tile + 1, pair) if 2 * tile + 1 < 5 else zero
            even = jnp.where(low_half, a, pltpu.roll(b, 64, 1))
            odd = jnp.where(low_half, pltpu.roll(a, 64, 1), b)
            for k, value in enumerate((even, odd)):
                row = tile * ROWS + base + 2 * pair + k
                fields[pl.ds(row, 8, stride=TILES * ROWS), :] = value


def force_kernel(
    extents,
    own,
    chip,
    far,
    body_force,
    residual,
    fields,
    windows,
    bonds,
    state,
    states,
    turn,
):
    column = lax.axis_index("gx")
    first = lax.axis_index("yz") * BLOCKS
    odd = lax.rem(column, 2)
    chip_base = jnp.where(odd == 0, 16, 0)
    far_base = 16 - chip_base
    other = 1 - odd

    flip = 4 * lax.rem(lax.axis_index("yz"), 2)
    stack = (flip, 1, 2, 3, 4 - flip)

    def lanes(pair):
        return pl.ds(128 * pair, 128)

    place(lambda b, p: own[pl.ds(stack[b], 1), :, lanes(p)][0], fields, 8)
    place(lambda b, p: chip[pl.ds(other * 5 + stack[b], 1), :, lanes(p)][0], fields, chip_base)
    place(lambda b, p: far[pl.ds(stack[b], 1), :, lanes(p)][0], fields, far_base + 2 * other, 3)

    span = TILES * ROWS
    row = lax.broadcasted_iota(jnp.int32, (span, 128), 0)
    lane72 = lax.broadcasted_iota(jnp.int32, (span, 128), 1)
    lattice = (
        (lax.rem(row, ROWS) - 8).astype(F32),
        (lax.div(row, ROWS) * 16 + lax.div(lane72, 8) - 8).astype(F32),
        lax.rem(lane72, 8).astype(F32),
    )

    def field(f):
        return pl.ds(f * span, span)

    for c in range(3):
        reference = fields[field(c), :] + lattice[c]
        if c == 2:
            reference = reference + 8.0 * fields[field(7), :]
        current = reference + fields[field(3 + c), :]
        fields[field(c), :] = reference * (1.0 / HORIZON)
        fields[field(3 + c), :] = current * (1.0 / HORIZON)
    along = column * 8 + lax.rem(row, ROWS) - 8
    across = first * 8 + lax.div(row, ROWS) * 16 + lax.div(lane72, 8) - 8
    inner = (along >= 0) & (along < extents[0] * 8) & (across >= 0) & (across < extents[1] * 8)
    fields[field(6), :] = jnp.where(inner, fields[field(6), :], 0.0)

    lane = lax.broadcasted_iota(jnp.int32, (8, 128), 1)
    z_of = lax.rem(lane, 8)

    def build(slot):
        dy, dz = SHIFTS[slot]
        back = 128 - (LANE0 + dy * 8 + dz)
        same = lane < back
        inside = (z_of + dz >= 0) & (z_of + dz < 8)

        def step(f, h):
            turned = [
                pltpu.roll(fields[pl.ds(f * span + t * ROWS + 8 * h, 8), :], back, 1)
                for t in range(TILES)
            ]
            for t in range(2):
                value = jnp.where(same, turned[t], turned[t + 1])
                if f == 6 and dz != 0:
                    value = jnp.where(inside, value, 0.0)
                windows[slot, f, t, pl.ds(8 * h, 8), :] = value

        return [functools.partial(step, f, h) for f in range(7) for h in range(ROWS // 8)]

    def spread(steps, part, parts):
        for step in steps[len(steps) * part // parts : len(steps) * (part + 1) // parts]:
            step()

    ahead = [step for slot in range(CENTRE) for step in build(slot)]
    progress = [0, 0]

    def advance(least):
        progress[0] += 1
        until = max(least, len(ahead) * progress[0] // (2 * (WIDE // 8) * BONDS))
        for step in ahead[progress[1] : until]:
            step()
        progress[1] = max(progress[1], until)

    patches = [(t, h) for t in range(2) for h in range(WIDE // 8)]
    starts, bond0 = [], 0
    for reach in REACHES:
        starts.append(bond0)
        bond0 += 2 * reach + 1

    def bond_sums(slot, sums):
        reach, bond = REACHES[slot], starts[slot]
        least = 0 if slot == CENTRE else 21 * (slot + 1)
        for n, (t, h) in enumerate(patches):
            at = pl.ds(8 * h, 8)
            p = [windows[CENTRE, c, t, pl.ds(8 - HALO + 8 * h, 8), :] for c in range(6)]
            for dx in range(-reach, reach + 1):
                advance(least)
                if dx == 0 and slot == CENTRE:
                    continue
                there = pl.ds(8 - HALO + 8 * h + dx, 8)
                d = [windows[slot, c, t, there, :] - p[c] for c in range(6)]
                r2 = d[0] * d[0] + d[1] * d[1] + d[2] * d[2]
                l2 = d[3] * d[3] + d[4] * d[4] + d[5] * d[5]
                over = lax.rsqrt(l2)
                r = r2 * lax.rsqrt(r2)
                length = l2 * over
                near = jnp.maximum(1.0 - r, 0.0)
                omega = near * near * windows[slot, 6, t, there, :]
                wr = omega * r
                sums[2 * n] = sums[2 * n] + wr * r
                sums[2 * n + 1] = sums[2 * n + 1] + wr * length
                bonds[bond + dx + reach, 0, t, at, :] = wr * over
                bonds[bond + dx + reach, 1, t, at, :] = omega

    zero = jnp.zeros((8, 128), F32)
    sums = [zero for _ in range(2 * len(patches))]
    order = [CENTRE] + list(range(CENTRE))
    spread(build(CENTRE), 0, 1)
    for slot in order:
        bond_sums(slot, sums)

    for n, (t, h) in enumerate(patches):
        scale = HORIZON * HORIZON
        kappa = 1.0 / jnp.maximum(scale * sums[2 * n], 1.0)
        theta = 3.0 * scale * (sums[2 * n + 1] - sums[2 * n]) * kappa
        pull = 225.0 * HORIZON * kappa
        state[0, t, pl.ds(8 * h, 8), :] = 105.0 * HORIZON * theta * kappa - pull
        state[1, t, pl.ds(8 * h, 8), :] = pull

    lane16 = lax.broadcasted_iota(jnp.int32, (WIDE, 128), 1)

    def build_state(slot):
        dy, dz = SHIFTS[slot]
        shift = dy * 8 + dz
        same = (lane16 + shift >= 0) & (lane16 + shift < 128)

        def step(k):
            turned = [pltpu.roll(state[k, t], -shift % 128, 1) for t in range(2)]
            for t in range(2):
                states[slot, k, t] = jnp.where(same, turned[t], turned[1 - t])

        return [functools.partial(step, k) for k in range(2)]

    own_rows = pl.ds(HALO, 8)

    def forces(slot, totals, beside):
        reach, bond = REACHES[slot], starts[slot]
        for t in range(2):
            spread(beside, t, 2)
            own_state = [state[k, t, own_rows, :] for k in range(2)]
            own_place = [windows[CENTRE, 3 + c, t, pl.ds(8, 8), :] for c in range(3)]
            for dx in range(-reach, reach + 1):
                if dx == 0 and slot == CENTRE:
                    continue
                there = pl.ds(HALO + dx, 8)
                theirs = [
                    (state[k, t, there, :] if slot == CENTRE else states[slot, k, t, there, :])
                    for k in range(2)
                ]
                slope, omega = (bonds[bond + dx + reach, k, t, own_rows, :] for k in range(2))
                scaled = slope * (own_state[0] + theirs[0]) + omega * (own_state[1] + theirs[1])
                for c in range(3):
                    y = windows[slot, 3 + c, t, pl.ds(8 + dx, 8), :] - own_place[c]
                    totals[3 * t + c] = totals[3 * t + c] + scaled * y

    totals = [zero for _ in range(6)]
    for slot, following in zip(order, order[1:] + [None]):
        forces(slot, totals, [] if following is None else build_state(following))

    lane8 = lax.broadcasted_iota(jnp.int32, (8, 128), 1)
    low_half = lax.broadcasted_iota(jnp.int32, (4, 128), 1) < 64
    for c in range(3):
        left, right = (pltpu.roll(totals[3 * t + c], 96, 1) for t in range(2))
        for n, source in enumerate((jnp.where(lane8 < 96, left, right), right)):
            turn[0] = source
            turn[1] = pltpu.roll(source, 64, 1)
            even, odd_row = pl.ds(0, 4, stride=2), pl.ds(1, 4, stride=2)
            for half in range(2 - n):
                b = 2 * n + half
                part = jnp.where(low_half, turn[half, even, :], turn[1 - half, odd_row, :])
                for pair in range(4):
                    at = lanes(pair)
                    value = part[pair : pair + 1, :] + body_force[b, c, :, at]
                    alive = own[1 + b, 6:7, at] > 0.0
                    residual[b, c, :, at] = jnp.where(alive, value, 0.0)


def permute(values, extent):
    lengths, heights = lax.axis_size("gx"), lax.axis_size("yz")
    table = []
    for g in range(lengths):
        for z in range(heights):
            dg, dz = extent(g, z)
            if 0 <= g + dg < lengths and 0 <= z + dz < heights:
                table.append((g * heights + z, (g + dg) * heights + z + dz))
    return lax.ppermute(values, AXES, table)


def run_force(extents, own5, chip, far, body_force):
    vmem = pl.BlockSpec(memory_space=pltpu.VMEM)
    points = own5.shape[-1]
    return pl.pallas_call(
        functools.partial(force_kernel, extents),
        out_shape=jax.ShapeDtypeStruct((BLOCKS, 3, 1, points), F32),
        in_specs=[vmem] * 4,
        out_specs=vmem,
        scratch_shapes=[
            pltpu.VMEM((FIELDS * TILES * ROWS, 128), F32),
            pltpu.VMEM((CENTRE + 1, 7, 2, ROWS, 128), F32),
            pltpu.VMEM((BONDS, 2, 2, WIDE, 128), F32),
            pltpu.VMEM((2, 2, WIDE, 128), F32),
            pltpu.VMEM((CENTRE, 2, 2, WIDE, 128), F32),
            pltpu.VMEM((2, 8, 128), F32),
        ],
        compiler_params=pltpu.CompilerParams(vmem_limit_bytes=24 * 1024 * 1024),
    )(own5, chip, far, body_force)


def flat(values):
    return jnp.moveaxis(values, 0, -2)


def body(jitter, displacement, volume, body_force, phase, counts, pair_list, pair_live):
    vmem = pl.BlockSpec(memory_space=pltpu.VMEM)
    points = volume.shape[-1]
    block = lambda n: jax.ShapeDtypeStruct((n, FIELDS, points), F32)
    own, edge_odd, edge_even = pl.pallas_call(
        pack_kernel,
        out_shape=(block(BLOCKS), block(1), block(1)),
        in_specs=[pl.BlockSpec(memory_space=pltpu.HBM)] * 5,
        out_specs=(vmem,) * 3,
        scratch_shapes=[
            pltpu.SMEM((8, counts.shape[1]), jnp.int32),
            pltpu.VMEM((BLOCKS, 3, 1, points), F32),
            pltpu.VMEM((BLOCKS, 3, 1, points), F32),
            pltpu.VMEM((BLOCKS, 1, points), F32),
            pltpu.VMEM((BLOCKS, 1, points), jnp.int32),
            pltpu.SemaphoreType.DMA((5,)),
        ],
        compiler_params=pltpu.CompilerParams(vmem_limit_bytes=60 * 1024 * 1024),
    )(counts, flat(jitter), flat(displacement), flat(volume), flat(phase))
    lengths, heights = lax.axis_size("gx"), lax.axis_size("yz")

    def device(g, z):
        return g * heights + z

    def pairs(couples):
        return [[device(*a), device(*b)] for a, b in couples]

    from_even = permute(edge_even, lambda g, z: (0, -1 if z % 2 else 1))
    couples = [((g, z), (g, z + 1)) for g in range(lengths) for z in range(1, heights - 1, 2)]
    couples += [((g, z), (g + 1, z)) for g in range(0, lengths, 2) for z in (0, heights - 1)]
    ends = lax.all_gather(edge_odd, AXES, axis=0, tiled=True, axis_index_groups=pairs(couples))
    odd = lax.rem(lax.axis_index("yz"), 2) == 1
    from_odd = jnp.where(odd, ends[1:], ends[:1])
    own5 = jnp.concatenate([from_odd, own, from_even], axis=0)
    cut = points // 4
    near_planes = jnp.where(
        lax.rem(lax.axis_index("gx"), 2) == 1, own5[:, :, cut:], own5[:, :, : points - cut]
    )
    far = permute(near_planes, lambda g, z: (1 if g % 2 else -1, 0))
    couples = [((g, z), (g + 1, z)) for g in range(0, lengths, 2) for z in range(heights)]
    chip = lax.all_gather(own5, AXES, axis=0, tiled=True, axis_index_groups=pairs(couples))
    residual = run_force(counts.shape, own5, chip, far, flat(body_force))
    return jnp.moveaxis(residual, 2, 0)


def solution(mesh):
    return jax.shard_map(
        body,
        mesh=mesh,
        in_specs=(
            P("gx", "yz", None, None),
            P("gx", "yz", None, None),
            P("gx", "yz", None),
            P("gx", "yz", None, None),
            P("gx", "yz", None),
            P(),
            P(("gx", "yz"), None),
            P(("gx", "yz")),
        ),
        out_specs=P("gx", "yz", None, None),
        check_vma=False,
    )
```

```python
import functools

import jax
import jax.numpy as jnp
from jax import lax
from jax.experimental import pallas as pl
from jax.experimental.pallas import tpu as pltpu
from jax.sharding import PartitionSpec as P

F32 = jnp.float32
AXES = ("gx", "yz")
BLOCKS = 3
ROWS = 24
TILES = 3
LANE0 = 32
HALO = 3
WIDE = 16
FIELDS = 8
HORIZON = 3.0


REACHES = (3,) * 8 + (2,) * 16 + (1,) * 12 + (3,)
CENTRE = len(REACHES) - 1
BONDS = sum(2 * reach + 1 for reach in REACHES)


def shifts():
    near = [(y, z) for y in (-1, 0, 1) for z in (-1, 0, 1) if (y, z) != (0, 0)]
    middle = [(y, z) for y in (-2, 2) for z in range(-2, 3)]
    middle += [(y, z) for y in (-1, 0, 1) for z in (-2, 2)]
    far = [(y, z) for y in (-3, 3) for z in (-1, 0, 1)]
    far += [(y, z) for z in (-3, 3) for y in (-1, 0, 1)]
    return near + middle + far + [(0, 0)]


SHIFTS = shifts()


def pack_kernel(
    counts,
    jitter,
    displacement,
    volume,
    phase,
    own,
    edge_odd,
    edge_even,
    count_row,
    jitters,
    displacements,
    volumes,
    phases,
    arrived,
):
    column = lax.axis_index("gx")
    place_z = lax.axis_index("yz")
    copies = [
        pltpu.make_async_copy(source, target, arrived.at[n])
        for n, (source, target) in enumerate(
            (
                (jitter, jitters),
                (displacement, displacements),
                (volume, volumes),
                (phase, phases),
                (counts.at[pl.ds(column // 8 * 8, 8)], count_row),
            )
        )
    ]
    for copy in copies:
        copy.start()
    for copy in copies:
        copy.wait()
    position = lax.broadcasted_iota(jnp.int32, (1, 512), 1)
    for b in range(BLOCKS):
        alive = position < count_row[lax.rem(column, 8), place_z * BLOCKS + b]
        for c in range(3):
            own[b, c : c + 1, :] = jitters[b, c]
            own[b, 3 + c : 4 + c, :] = displacements[b, c]
        own[b, 6:7, :] = jnp.where(alive, volumes[b], 0.0)
        own[b, 7:8, :] = phases[b].astype(F32)
    odd = lax.rem(place_z, 2) == 1
    first, last = own[0], own[BLOCKS - 1]
    edge_odd[0] = jnp.where(odd, last, first)
    edge_even[0] = jnp.where(odd, first, last)


def place(block_of, fields, base, pairs=4):
    lane = lax.broadcasted_iota(jnp.int32, (8, 128), 1)
    low_half = lane < 64
    zero = jnp.zeros((8, 128), F32)
    for pair in range(pairs):
        for tile in range(TILES):
            a = block_of(2 * tile, pair)
            b = block_of(2 * tile + 1, pair) if 2 * tile + 1 < 5 else zero
            even = jnp.where(low_half, a, pltpu.roll(b, 64, 1))
            odd = jnp.where(low_half, pltpu.roll(a, 64, 1), b)
            for k, value in enumerate((even, odd)):
                row = tile * ROWS + base + 2 * pair + k
                fields[pl.ds(row, 8, stride=TILES * ROWS), :] = value


def force_kernel(
    extents,
    own,
    chip,
    far,
    body_force,
    residual,
    fields,
    windows,
    bonds,
    state,
    states,
    turn,
):
    column = lax.axis_index("gx")
    first = lax.axis_index("yz") * BLOCKS
    odd = lax.rem(column, 2)
    chip_base = jnp.where(odd == 0, 16, 0)
    far_base = 16 - chip_base
    other = 1 - odd

    flip = 4 * lax.rem(lax.axis_index("yz"), 2)
    stack = (flip, 1, 2, 3, 4 - flip)

    def lanes(pair):
        return pl.ds(128 * pair, 128)

    place(lambda b, p: own[pl.ds(stack[b], 1), :, lanes(p)][0], fields, 8)
    place(lambda b, p: chip[pl.ds(other * 5 + stack[b], 1), :, lanes(p)][0], fields, chip_base)
    place(lambda b, p: far[pl.ds(stack[b], 1), :, lanes(p)][0], fields, far_base + 2 * other, 3)

    span = TILES * ROWS
    row = lax.broadcasted_iota(jnp.int32, (span, 128), 0)
    lane72 = lax.broadcasted_iota(jnp.int32, (span, 128), 1)
    lattice = (
        (lax.rem(row, ROWS) - 8).astype(F32),
        (lax.div(row, ROWS) * 16 + lax.div(lane72, 8) - 8).astype(F32),
        lax.rem(lane72, 8).astype(F32),
    )

    def field(f):
        return pl.ds(f * span, span)

    for c in range(3):
        reference = fields[field(c), :] + lattice[c]
        if c == 2:
            reference = reference + 8.0 * fields[field(7), :]
        current = reference + fields[field(3 + c), :]
        fields[field(c), :] = reference * (1.0 / HORIZON)
        fields[field(3 + c), :] = current * (1.0 / HORIZON)
    along = column * 8 + lax.rem(row, ROWS) - 8
    across = first * 8 + lax.div(row, ROWS) * 16 + lax.div(lane72, 8) - 8
    inner = (along >= 0) & (along < extents[0] * 8) & (across >= 0) & (across < extents[1] * 8)
    fields[field(6), :] = jnp.where(inner, fields[field(6), :], 0.0)

    lane = lax.broadcasted_iota(jnp.int32, (8, 128), 1)
    z_of = lax.rem(lane, 8)

    def build(slot):
        dy, dz = SHIFTS[slot]
        back = 128 - (LANE0 + dy * 8 + dz)
        same = lane < back
        inside = (z_of + dz >= 0) & (z_of + dz < 8)

        def step(f, h):
            turned = [
                pltpu.roll(fields[pl.ds(f * span + t * ROWS + 8 * h, 8), :], back, 1)
                for t in range(TILES)
            ]
            for t in range(2):
                value = jnp.where(same, turned[t], turned[t + 1])
                if f == 6 and dz != 0:
                    value = jnp.where(inside, value, 0.0)
                windows[slot, f, t, pl.ds(8 * h, 8), :] = value

        return [functools.partial(step, f, h) for f in range(7) for h in range(ROWS // 8)]

    def spread(steps, part, parts):
        for step in steps[len(steps) * part // parts : len(steps) * (part + 1) // parts]:
            step()

    ahead = [step for slot in range(CENTRE) for step in build(slot)]
    progress = [0, 0]

    def advance(least):
        progress[0] += 1
        until = max(least, len(ahead) * progress[0] // (2 * (WIDE // 8) * BONDS))
        for step in ahead[progress[1] : until]:
            step()
        progress[1] = max(progress[1], until)

    patches = [(t, h) for t in range(2) for h in range(WIDE // 8)]
    starts, bond0 = [], 0
    for reach in REACHES:
        starts.append(bond0)
        bond0 += 2 * reach + 1

    def bond_sums(slot, sums):
        reach, bond = REACHES[slot], starts[slot]
        least = 0 if slot == CENTRE else 21 * (slot + 1)
        for n, (t, h) in enumerate(patches):
            at = pl.ds(8 * h, 8)
            p = [windows[CENTRE, c, t, pl.ds(8 - HALO + 8 * h, 8), :] for c in range(6)]
            for dx in range(-reach, reach + 1):
                advance(least)
                if dx == 0 and slot == CENTRE:
                    continue
                there = pl.ds(8 - HALO + 8 * h + dx, 8)
                d = [windows[slot, c, t, there, :] - p[c] for c in range(6)]
                r2 = d[0] * d[0] + d[1] * d[1] + d[2] * d[2]
                l2 = d[3] * d[3] + d[4] * d[4] + d[5] * d[5]
                over = lax.rsqrt(l2)
                r = r2 * lax.rsqrt(r2)
                length = l2 * over
                near = jnp.maximum(1.0 - r, 0.0)
                omega = near * near * windows[slot, 6, t, there, :]
                wr = omega * r
                sums[2 * n] = sums[2 * n] + wr * r
                sums[2 * n + 1] = sums[2 * n + 1] + wr * length
                bonds[bond + dx + reach, 0, t, at, :] = wr * over
                bonds[bond + dx + reach, 1, t, at, :] = omega

    zero = jnp.zeros((8, 128), F32)
    sums = [zero for _ in range(2 * len(patches))]
    order = [CENTRE] + list(range(CENTRE))
    spread(build(CENTRE), 0, 1)
    for slot in order:
        bond_sums(slot, sums)

    for n, (t, h) in enumerate(patches):
        scale = HORIZON * HORIZON
        kappa = 1.0 / jnp.maximum(scale * sums[2 * n], 1.0)
        theta = 3.0 * scale * (sums[2 * n + 1] - sums[2 * n]) * kappa
        pull = 225.0 * HORIZON * kappa
        state[0, t, pl.ds(8 * h, 8), :] = 105.0 * HORIZON * theta * kappa - pull
        state[1, t, pl.ds(8 * h, 8), :] = pull

    lane16 = lax.broadcasted_iota(jnp.int32, (WIDE, 128), 1)

    def build_state(slot):
        dy, dz = SHIFTS[slot]
        shift = dy * 8 + dz
        same = (lane16 + shift >= 0) & (lane16 + shift < 128)

        def step(k):
            turned = [pltpu.roll(state[k, t], -shift % 128, 1) for t in range(2)]
            for t in range(2):
                states[slot, k, t] = jnp.where(same, turned[t], turned[1 - t])

        return [functools.partial(step, k) for k in range(2)]

    own_rows = pl.ds(HALO, 8)

    def forces(slot, totals, beside):
        reach, bond = REACHES[slot], starts[slot]
        for t in range(2):
            spread(beside, t, 2)
            own_state = [state[k, t, own_rows, :] for k in range(2)]
            own_place = [windows[CENTRE, 3 + c, t, pl.ds(8, 8), :] for c in range(3)]
            for dx in range(-reach, reach + 1):
                if dx == 0 and slot == CENTRE:
                    continue
                there = pl.ds(HALO + dx, 8)
                theirs = [
                    (state[k, t, there, :] if slot == CENTRE else states[slot, k, t, there, :])
                    for k in range(2)
                ]
                slope, omega = (bonds[bond + dx + reach, k, t, own_rows, :] for k in range(2))
                scaled = slope * (own_state[0] + theirs[0]) + omega * (own_state[1] + theirs[1])
                for c in range(3):
                    y = windows[slot, 3 + c, t, pl.ds(8 + dx, 8), :] - own_place[c]
                    totals[3 * t + c] = totals[3 * t + c] + scaled * y

    totals = [zero for _ in range(6)]
    for slot, following in zip(order, order[1:] + [None]):
        forces(slot, totals, [] if following is None else build_state(following))

    lane8 = lax.broadcasted_iota(jnp.int32, (8, 128), 1)
    low_half = lax.broadcasted_iota(jnp.int32, (4, 128), 1) < 64
    for c in range(3):
        left, right = (pltpu.roll(totals[3 * t + c], 96, 1) for t in range(2))
        for n, source in enumerate((jnp.where(lane8 < 96, left, right), right)):
            turn[0] = source
            turn[1] = pltpu.roll(source, 64, 1)
            even, odd_row = pl.ds(0, 4, stride=2), pl.ds(1, 4, stride=2)
            for half in range(2 - n):
                b = 2 * n + half
                part = jnp.where(low_half, turn[half, even, :], turn[1 - half, odd_row, :])
                for pair in range(4):
                    at = lanes(pair)
                    value = part[pair : pair + 1, :] + body_force[b, c, :, at]
                    alive = own[1 + b, 6:7, at] > 0.0
                    residual[b, c, :, at] = jnp.where(alive, value, 0.0)


def permute(values, extent):
    lengths, heights = lax.axis_size("gx"), lax.axis_size("yz")
    table = []
    for g in range(lengths):
        for z in range(heights):
            dg, dz = extent(g, z)
            if 0 <= g + dg < lengths and 0 <= z + dz < heights:
                table.append((g * heights + z, (g + dg) * heights + z + dz))
    return lax.ppermute(values, AXES, table)


def run_force(extents, own5, chip, far, body_force):
    vmem = pl.BlockSpec(memory_space=pltpu.VMEM)
    points = own5.shape[-1]
    return pl.pallas_call(
        functools.partial(force_kernel, extents),
        out_shape=jax.ShapeDtypeStruct((BLOCKS, 3, 1, points), F32),
        in_specs=[vmem] * 4,
        out_specs=vmem,
        scratch_shapes=[
            pltpu.VMEM((FIELDS * TILES * ROWS, 128), F32),
            pltpu.VMEM((CENTRE + 1, 7, 2, ROWS, 128), F32),
            pltpu.VMEM((BONDS, 2, 2, WIDE, 128), F32),
            pltpu.VMEM((2, 2, WIDE, 128), F32),
            pltpu.VMEM((CENTRE, 2, 2, WIDE, 128), F32),
            pltpu.VMEM((2, 8, 128), F32),
        ],
        compiler_params=pltpu.CompilerParams(vmem_limit_bytes=24 * 1024 * 1024),
    )(own5, chip, far, body_force)


def flat(values):
    return jnp.moveaxis(values, 0, -2)


def body(jitter, displacement, volume, body_force, phase, counts, pair_list, pair_live):
    vmem = pl.BlockSpec(memory_space=pltpu.VMEM)
    points = volume.shape[-1]
    block = lambda n: jax.ShapeDtypeStruct((n, FIELDS, points), F32)
    own, edge_odd, edge_even = pl.pallas_call(
        pack_kernel,
        out_shape=(block(BLOCKS), block(1), block(1)),
        in_specs=[pl.BlockSpec(memory_space=pltpu.HBM)] * 5,
        out_specs=(vmem,) * 3,
        scratch_shapes=[
            pltpu.SMEM((8, counts.shape[1]), jnp.int32),
            pltpu.VMEM((BLOCKS, 3, 1, points), F32),
            pltpu.VMEM((BLOCKS, 3, 1, points), F32),
            pltpu.VMEM((BLOCKS, 1, points), F32),
            pltpu.VMEM((BLOCKS, 1, points), jnp.int32),
            pltpu.SemaphoreType.DMA((5,)),
        ],
        compiler_params=pltpu.CompilerParams(vmem_limit_bytes=60 * 1024 * 1024),
    )(counts, flat(jitter), flat(displacement), flat(volume), flat(phase))
    lengths, heights = lax.axis_size("gx"), lax.axis_size("yz")

    def device(g, z):
        return g * heights + z

    def pairs(couples):
        return [[device(*a), device(*b)] for a, b in couples]

    from_odd = permute(edge_odd, lambda g, z: (0, 1 if z % 2 else -1))
    couples = [((g, z), (g, z + 1)) for g in range(lengths) for z in range(0, heights, 2)]
    ends = lax.all_gather(edge_even, AXES, axis=0, tiled=True, axis_index_groups=pairs(couples))
    odd = lax.rem(lax.axis_index("yz"), 2) == 1
    from_even = jnp.where(odd, ends[:1], ends[1:])
    own5 = jnp.concatenate([from_odd, own, from_even], axis=0)
    cut = points // 4
    near_planes = jnp.where(
        lax.rem(lax.axis_index("gx"), 2) == 1, own5[:, :, cut:], own5[:, :, : points - cut]
    )
    far = permute(near_planes, lambda g, z: (1 if g % 2 else -1, 0))
    couples = [((g, z), (g + 1, z)) for g in range(0, lengths, 2) for z in range(heights)]
    chip = lax.all_gather(own5, AXES, axis=0, tiled=True, axis_index_groups=pairs(couples))
    residual = run_force(counts.shape, own5, chip, far, flat(body_force))
    return jnp.moveaxis(residual, 2, 0)


def solution(mesh):
    return jax.shard_map(
        body,
        mesh=mesh,
        in_specs=(
            P("gx", "yz", None, None),
            P("gx", "yz", None, None),
            P("gx", "yz", None),
            P("gx", "yz", None, None),
            P("gx", "yz", None),
            P(),
            P(("gx", "yz"), None),
            P(("gx", "yz")),
        ),
        out_specs=P("gx", "yz", None, None),
        check_vma=False,
    )
```

```python
import functools

import jax
import jax.numpy as jnp
from jax import lax
from jax.experimental import pallas as pl
from jax.experimental.pallas import tpu as pltpu
from jax.sharding import PartitionSpec as P

F32 = jnp.float32
AXES = ("gx", "yz")
BLOCKS = 3
ROWS = 24
TILES = 3
LANE0 = 32
HALO = 3
WIDE = 16
FIELDS = 8
HORIZON = 3.0


REACHES = (3,) * 8 + (2,) * 16 + (1,) * 12 + (3,)
CENTRE = len(REACHES) - 1
BONDS = sum(2 * reach + 1 for reach in REACHES)


def shifts():
    near = [(y, z) for y in (-1, 0, 1) for z in (-1, 0, 1) if (y, z) != (0, 0)]
    middle = [(y, z) for y in (-2, 2) for z in range(-2, 3)]
    middle += [(y, z) for y in (-1, 0, 1) for z in (-2, 2)]
    far = [(y, z) for y in (-3, 3) for z in (-1, 0, 1)]
    far += [(y, z) for z in (-3, 3) for y in (-1, 0, 1)]
    return near + middle + far + [(0, 0)]


SHIFTS = shifts()


def pack_kernel(
    counts,
    jitter,
    displacement,
    volume,
    phase,
    own,
    edge_odd,
    edge_even,
    count_row,
    jitters,
    displacements,
    volumes,
    phases,
    arrived,
):
    column = lax.axis_index("gx")
    place_z = lax.axis_index("yz")
    copies = [
        pltpu.make_async_copy(source, target, arrived.at[n])
        for n, (source, target) in enumerate(
            (
                (jitter, jitters),
                (displacement, displacements),
                (volume, volumes),
                (phase, phases),
                (counts.at[pl.ds(column // 8 * 8, 8)], count_row),
            )
        )
    ]
    for copy in copies:
        copy.start()
    for copy in copies:
        copy.wait()
    position = lax.broadcasted_iota(jnp.int32, (1, 512), 1)
    for b in range(BLOCKS):
        alive = position < count_row[lax.rem(column, 8), place_z * BLOCKS + b]
        for c in range(3):
            own[b, c : c + 1, :] = jitters[b, c]
            own[b, 3 + c : 4 + c, :] = displacements[b, c]
        own[b, 6:7, :] = jnp.where(alive, volumes[b], 0.0)
        own[b, 7:8, :] = phases[b].astype(F32)
    odd = lax.rem(place_z, 2) == 1
    first, last = own[0], own[BLOCKS - 1]
    edge_odd[0] = jnp.where(odd, last, first)
    edge_even[0] = jnp.where(odd, first, last)


def place(block_of, fields, base, pairs=4):
    lane = lax.broadcasted_iota(jnp.int32, (8, 128), 1)
    low_half = lane < 64
    zero = jnp.zeros((8, 128), F32)
    for pair in range(pairs):
        for tile in range(TILES):
            a = block_of(2 * tile, pair)
            b = block_of(2 * tile + 1, pair) if 2 * tile + 1 < 5 else zero
            even = jnp.where(low_half, a, pltpu.roll(b, 64, 1))
            odd = jnp.where(low_half, pltpu.roll(a, 64, 1), b)
            for k, value in enumerate((even, odd)):
                row = tile * ROWS + base + 2 * pair + k
                fields[pl.ds(row, 8, stride=TILES * ROWS), :] = value


def force_kernel(
    own,
    chip,
    far,
    body_force,
    residual,
    fields,
    windows,
    bonds,
    state,
    states,
    turn,
):
    column = lax.axis_index("gx")
    first = lax.axis_index("yz") * BLOCKS
    odd = lax.rem(column, 2)
    chip_base = jnp.where(odd == 0, 16, 0)
    far_base = 16 - chip_base
    other = 1 - odd

    flip = 4 * lax.rem(lax.axis_index("yz"), 2)
    stack = (flip, 1, 2, 3, 4 - flip)

    def lanes(pair):
        return pl.ds(128 * pair, 128)

    place(lambda b, p: own[pl.ds(stack[b], 1), :, lanes(p)][0], fields, 8)
    place(lambda b, p: chip[pl.ds(other * 5 + stack[b], 1), :, lanes(p)][0], fields, chip_base)
    place(lambda b, p: far[pl.ds(stack[b], 1), :, lanes(p)][0], fields, far_base + 2 * other, 3)

    span = TILES * ROWS
    row = lax.broadcasted_iota(jnp.int32, (ROWS, 128), 0)
    lane24 = lax.broadcasted_iota(jnp.int32, (ROWS, 128), 1)
    for t in range(TILES):
        lattice = (
            (row - 8).astype(F32),
            ((lane24 >> 3) + (16 * t - 8)).astype(F32),
            (lane24 & 7).astype(F32),
        )

        def field(f, t=t):
            return pl.ds(f * span + t * ROWS, ROWS)

        for c in range(3):
            reference = fields[field(c), :] + lattice[c]
            if c == 2:
                reference = reference + 8.0 * fields[field(7), :]
            current = reference + fields[field(3 + c), :]
            fields[field(c), :] = reference * (1.0 / HORIZON)
            fields[field(3 + c), :] = current * (1.0 / HORIZON)

    lane = lax.broadcasted_iota(jnp.int32, (8, 128), 1)
    z_of = lane & 7

    def build(slot):
        dy, dz = SHIFTS[slot]
        back = 128 - (LANE0 + dy * 8 + dz)
        same = lane < back
        inside = (z_of + dz >= 0) & (z_of + dz < 8)

        def step(f, h):
            turned = [
                pltpu.roll(fields[pl.ds(f * span + t * ROWS + 8 * h, 8), :], back, 1)
                for t in range(TILES)
            ]
            for t in range(2):
                value = jnp.where(same, turned[t], turned[t + 1])
                if f == 6 and dz != 0:
                    value = jnp.where(inside, value, 0.0)
                windows[slot, f, t, pl.ds(8 * h, 8), :] = value

        return [functools.partial(step, f, h) for f in range(7) for h in range(ROWS // 8)]

    def spread(steps, part, parts):
        for step in steps[len(steps) * part // parts : len(steps) * (part + 1) // parts]:
            step()

    ahead = [step for slot in range(CENTRE) for step in build(slot)]
    progress = [0, 0]

    def advance(least):
        progress[0] += 1
        until = max(least, len(ahead) * progress[0] // (2 * (WIDE // 8) * BONDS))
        for step in ahead[progress[1] : until]:
            step()
        progress[1] = max(progress[1], until)

    patches = [(t, h) for t in range(2) for h in range(WIDE // 8)]
    starts, bond0 = [], 0
    for reach in REACHES:
        starts.append(bond0)
        bond0 += 2 * reach + 1

    def bond_sums(slot, sums):
        reach, bond = REACHES[slot], starts[slot]
        least = 0 if slot == CENTRE else 21 * (slot + 1)
        for n, (t, h) in enumerate(patches):
            at = pl.ds(8 * h, 8)
            p = [windows[CENTRE, c, t, pl.ds(8 - HALO + 8 * h, 8), :] for c in range(6)]
            for dx in range(-reach, reach + 1):
                advance(least)
                if dx == 0 and slot == CENTRE:
                    continue
                there = pl.ds(8 - HALO + 8 * h + dx, 8)
                d = [windows[slot, c, t, there, :] - p[c] for c in range(6)]
                r2 = d[0] * d[0] + d[1] * d[1] + d[2] * d[2]
                l2 = d[3] * d[3] + d[4] * d[4] + d[5] * d[5]
                over = lax.rsqrt(l2)
                r = r2 * lax.rsqrt(r2)
                length = l2 * over
                near = jnp.maximum(1.0 - r, 0.0)
                omega = near * near * windows[slot, 6, t, there, :]
                wr = omega * r
                sums[2 * n] = sums[2 * n] + wr * r
                sums[2 * n + 1] = sums[2 * n + 1] + wr * length
                bonds[bond + dx + reach, 0, t, at, :] = wr * over
                bonds[bond + dx + reach, 1, t, at, :] = omega

    zero = jnp.zeros((8, 128), F32)
    sums = [zero for _ in range(2 * len(patches))]
    order = [CENTRE] + list(range(CENTRE))
    spread(build(CENTRE), 0, 1)
    for slot in order:
        bond_sums(slot, sums)

    for n, (t, h) in enumerate(patches):
        scale = HORIZON * HORIZON
        kappa = 1.0 / jnp.maximum(scale * sums[2 * n], 1.0)
        theta = 3.0 * scale * (sums[2 * n + 1] - sums[2 * n]) * kappa
        pull = 225.0 * HORIZON * kappa
        state[0, t, pl.ds(8 * h, 8), :] = 105.0 * HORIZON * theta * kappa - pull
        state[1, t, pl.ds(8 * h, 8), :] = pull

    lane16 = lax.broadcasted_iota(jnp.int32, (WIDE, 128), 1)

    def build_state(slot):
        dy, dz = SHIFTS[slot]
        shift = dy * 8 + dz
        same = (lane16 + shift >= 0) & (lane16 + shift < 128)

        def step(k):
            turned = [pltpu.roll(state[k, t], -shift % 128, 1) for t in range(2)]
            for t in range(2):
                states[slot, k, t] = jnp.where(same, turned[t], turned[1 - t])

        return [functools.partial(step, k) for k in range(2)]

    own_rows = pl.ds(HALO, 8)

    def forces(slot, totals, beside):
        reach, bond = REACHES[slot], starts[slot]
        for t in range(2):
            spread(beside, t, 2)
            own_state = [state[k, t, own_rows, :] for k in range(2)]
            own_place = [windows[CENTRE, 3 + c, t, pl.ds(8, 8), :] for c in range(3)]
            for dx in range(-reach, reach + 1):
                if dx == 0 and slot == CENTRE:
                    continue
                there = pl.ds(HALO + dx, 8)
                theirs = [
                    (state[k, t, there, :] if slot == CENTRE else states[slot, k, t, there, :])
                    for k in range(2)
                ]
                slope, omega = (bonds[bond + dx + reach, k, t, own_rows, :] for k in range(2))
                scaled = slope * (own_state[0] + theirs[0]) + omega * (own_state[1] + theirs[1])
                for c in range(3):
                    y = windows[slot, 3 + c, t, pl.ds(8 + dx, 8), :] - own_place[c]
                    totals[3 * t + c] = totals[3 * t + c] + scaled * y

    totals = [zero for _ in range(6)]
    for slot, following in zip(order, order[1:] + [None]):
        forces(slot, totals, [] if following is None else build_state(following))

    lane8 = lax.broadcasted_iota(jnp.int32, (8, 128), 1)
    low_half = lax.broadcasted_iota(jnp.int32, (4, 128), 1) < 64
    for c in range(3):
        left, right = (pltpu.roll(totals[3 * t + c], 96, 1) for t in range(2))
        for n, source in enumerate((jnp.where(lane8 < 96, left, right), right)):
            turn[0] = source
            turn[1] = pltpu.roll(source, 64, 1)
            even, odd_row = pl.ds(0, 4, stride=2), pl.ds(1, 4, stride=2)
            for half in range(2 - n):
                b = 2 * n + half
                part = jnp.where(low_half, turn[half, even, :], turn[1 - half, odd_row, :])
                for pair in range(4):
                    at = lanes(pair)
                    value = part[pair : pair + 1, :] + body_force[b, c, :, at]
                    alive = own[1 + b, 6:7, at] > 0.0
                    residual[b, c, :, at] = jnp.where(alive, value, 0.0)


def permute(values, extent):
    lengths, heights = lax.axis_size("gx"), lax.axis_size("yz")
    table = []
    for g in range(lengths):
        for z in range(heights):
            dg, dz = extent(g, z)
            if 0 <= g + dg < lengths and 0 <= z + dz < heights:
                table.append((g * heights + z, (g + dg) * heights + z + dz))
    return lax.ppermute(values, AXES, table)


def run_force(own5, chip, far, body_force):
    vmem = pl.BlockSpec(memory_space=pltpu.VMEM)
    points = own5.shape[-1]
    return pl.pallas_call(
        force_kernel,
        out_shape=jax.ShapeDtypeStruct((BLOCKS, 3, 1, points), F32),
        in_specs=[vmem] * 4,
        out_specs=vmem,
        scratch_shapes=[
            pltpu.VMEM((FIELDS * TILES * ROWS, 128), F32),
            pltpu.VMEM((CENTRE + 1, 7, 2, ROWS, 128), F32),
            pltpu.VMEM((BONDS, 2, 2, WIDE, 128), F32),
            pltpu.VMEM((2, 2, WIDE, 128), F32),
            pltpu.VMEM((CENTRE, 2, 2, WIDE, 128), F32),
            pltpu.VMEM((2, 8, 128), F32),
        ],
        compiler_params=pltpu.CompilerParams(vmem_limit_bytes=24 * 1024 * 1024),
    )(own5, chip, far, body_force)


def flat(values):
    return jnp.moveaxis(values, 0, -2)


def body(jitter, displacement, volume, body_force, phase, counts, pair_list, pair_live):
    vmem = pl.BlockSpec(memory_space=pltpu.VMEM)
    points = volume.shape[-1]
    block = lambda n: jax.ShapeDtypeStruct((n, FIELDS, points), F32)
    own, edge_odd, edge_even = pl.pallas_call(
        pack_kernel,
        out_shape=(block(BLOCKS), block(1), block(1)),
        in_specs=[pl.BlockSpec(memory_space=pltpu.HBM)] * 5,
        out_specs=(vmem,) * 3,
        scratch_shapes=[
            pltpu.SMEM((8, counts.shape[1]), jnp.int32),
            pltpu.VMEM((BLOCKS, 3, 1, points), F32),
            pltpu.VMEM((BLOCKS, 3, 1, points), F32),
            pltpu.VMEM((BLOCKS, 1, points), F32),
            pltpu.VMEM((BLOCKS, 1, points), jnp.int32),
            pltpu.SemaphoreType.DMA((5,)),
        ],
        compiler_params=pltpu.CompilerParams(vmem_limit_bytes=60 * 1024 * 1024),
    )(counts, flat(jitter), flat(displacement), flat(volume), flat(phase))
    lengths, heights = lax.axis_size("gx"), lax.axis_size("yz")

    def device(g, z):
        return g * heights + z

    def pairs(couples):
        return [[device(*a), device(*b)] for a, b in couples]

    from_odd = permute(edge_odd, lambda g, z: (0, 1 if z % 2 else -1))
    couples = [((g, z), (g, z + 1)) for g in range(lengths) for z in range(0, heights, 2)]
    ends = lax.all_gather(edge_even, AXES, axis=0, tiled=True, axis_index_groups=pairs(couples))
    odd = lax.rem(lax.axis_index("yz"), 2) == 1
    from_even = jnp.where(odd, ends[:1], ends[1:])
    own5 = jnp.concatenate([from_odd, own, from_even], axis=0)
    cut = points // 4
    near_planes = jnp.where(
        lax.rem(lax.axis_index("gx"), 2) == 1, own5[:, :, cut:], own5[:, :, : points - cut]
    )
    far = permute(near_planes, lambda g, z: (1 if g % 2 else -1, 0))
    couples = [((g, z), (g + 1, z)) for g in range(0, lengths, 2) for z in range(heights)]
    chip = lax.all_gather(own5, AXES, axis=0, tiled=True, axis_index_groups=pairs(couples))
    residual = run_force(own5, chip, far, flat(body_force))
    return jnp.moveaxis(residual, 2, 0)


def solution(mesh):
    return jax.shard_map(
        body,
        mesh=mesh,
        in_specs=(
            P("gx", "yz", None, None),
            P("gx", "yz", None, None),
            P("gx", "yz", None),
            P("gx", "yz", None, None),
            P("gx", "yz", None),
            P(),
            P(("gx", "yz"), None),
            P(("gx", "yz")),
        ),
        out_specs=P("gx", "yz", None, None),
        check_vma=False,
    )
```
